32 devices in a mesh: mem: 4 (over y, x), tile: 8 (over z, core).
Axes of the slice: x: 2, y: 2, z: 4, core: 2. Of those that a mesh axis runs over, the one named last changes fastest.
Arguments:
- perturbations: bfloat16 [20, 32, 24, 192], P('mem', None, 'tile'), may hold values from -6 to 6
- control: float32 [20, 32, 24, 192], P('mem', None, 'tile'), may hold values from -6 to 6
- filter_rate: float32 [24, 32], P('tile'), may hold values from 0.45 to 1, as said below
- lat_weight: int32 [48], P('tile'), may hold values from 0 to 256
- lon_weight: int32 [384], replicated, may hold values from 0 to 256
- wind_east: int32 [48, 384], P(None, 'tile'), may hold values from -480 to 480
- wind_north: int32 [48, 384], P(None, 'tile'), may hold values from -480 to 480
- obs_weight: float32 [32, 48, 384], P(None, None, 'tile'), may hold values from 1 to 16
Outputs:
- hessian_product: float32 [20, 32, 24, 192], P('mem', None, 'tile')
The draws below stay inside these ranges and needn't reach their ends.
Inputs may be any that keep to these rules, and one draw needn't show every extreme that they name: `filter_rate`: every rate lies strictly below 1.
All inputs are finite; a program needn't handle non-finite values.
Results may differ from the reference program's by a relative error of at most 0.0003.
Values sent between devices are 32-bit elements; how exact they have to be, the bound alone decides.
A program may use at most 64 MiB of HBM per device.

```python
import math
import jax
import jax.numpy as jnp
from jax import lax

QUANTITY_HEIGHTS = 32
MEMBERS = 20
NC = 192
STEPS = 3
LOWRES_LAT_TOTAL = 24
ROWS_F = 48
COLS_F = 384


def draw_filter_rate(key, part):
    speed_stream_seed, picking_seed, latitude_stream_seed, spike_stream_seed, wobble_stream_seed = jax.random.split(jax.random.fold_in(key, 17), 5)
    uniform_vals = jax.random.uniform(speed_stream_seed, (QUANTITY_HEIGHTS,), dtype=jnp.float32)
    slow_mask = jax.random.uniform(picking_seed, (QUANTITY_HEIGHTS,), dtype=jnp.float32) < 0.5
    slow_gap = (0.2 + 0.4 * uniform_vals) / LOWRES_LAT_TOTAL
    fast_gap = 1.0 / (12.0 + 38.0 * uniform_vals)
    gap_vals = jnp.where(slow_mask, slow_gap, fast_gap)
    jitter = jax.random.uniform(wobble_stream_seed, (LOWRES_LAT_TOTAL, QUANTITY_HEIGHTS), dtype=jnp.float32, minval=0.5, maxval=2.0)
    base_rate = 1.0 - gap_vals[None, :] * jitter
    positions = jax.random.randint(latitude_stream_seed, (3,), 0, LOWRES_LAT_TOTAL)
    row_ids = jnp.arange(LOWRES_LAT_TOTAL)
    struck = jnp.any(row_ids[:, None] == positions[None, :], axis=1)
    threshold_numbers = jax.random.uniform(spike_stream_seed, (LOWRES_LAT_TOTAL, QUANTITY_HEIGHTS), dtype=jnp.float32, minval=0.6, maxval=0.8)
    return jnp.where(struck[:, None], base_rate * threshold_numbers, base_rate).astype(jnp.float32)


def with_ends(values, key, least, largest):
    index_at = [jax.random.randint(jax.random.fold_in(key, axis), (), 0, length) for axis, length in enumerate(values.shape)]
    longest = values.shape.index(max(values.shape))
    beside = index_at[:longest] + [(index_at[longest] + 1) % values.shape[longest]] + index_at[longest + 1:]
    return values.at[tuple(index_at)].set(least).at[tuple(beside)].set(largest)


def block_scale(key, shape, cuts, smallest, high):
    def one(axis_at, blocks):
        heights = jax.random.uniform(jax.random.fold_in(jax.random.fold_in(key, 6), axis_at), (blocks,), jnp.float32, smallest / len(cuts), high / len(cuts))
        return jnp.repeat(jnp.exp(heights), shape[axis_at] // blocks).reshape((-1,) + (1,) * (len(shape) - axis_at - 1))

    gain = one(*cuts[0])
    for cut in cuts[1:]:
        gain = gain * one(*cut)
    return gain


def bell_draw(own_key, extent, width, reach, cuts=(), held_as=jnp.bfloat16):
    level = block_scale(own_key, extent, cuts, -0.22, 0.18) if cuts else 1.0
    values = jax.random.normal(own_key, extent, jnp.float32) * width * level
    return jnp.minimum(jnp.maximum(values, -reach), reach).astype(held_as)


def setup_inputs(seed: int = 0) -> dict:
    splits = jax.random.split(jax.random.key(seed), 9)
    return {
        "perturbations": bell_draw(splits[0], (MEMBERS, QUANTITY_HEIGHTS, LOWRES_LAT_TOTAL, NC), 1.0, 6.0, ((0, 4), (2, 8))),
        "control": bell_draw(splits[1], (MEMBERS, QUANTITY_HEIGHTS, LOWRES_LAT_TOTAL, NC), 1.0, 6.0, ((0, 4), (2, 8)), jnp.float32),
        "filter_rate": draw_filter_rate(jax.random.fold_in(splits[8], 71), 0),
        "lat_weight": with_ends(jax.random.randint(splits[3], (ROWS_F,), 0, 257), jax.random.fold_in(splits[3], 1), 0, 256).astype(jnp.int32),
        "lon_weight": with_ends(jax.random.randint(splits[4], (COLS_F,), 0, 257), jax.random.fold_in(splits[4], 1), 0, 256).astype(jnp.int32),
        "wind_east": with_ends(jax.random.randint(splits[5], (ROWS_F, COLS_F), -480, 481), jax.random.fold_in(splits[5], 1), -480, 480).astype(jnp.int32),
        "wind_north": with_ends(jax.random.randint(splits[6], (ROWS_F, COLS_F), -480, 481), jax.random.fold_in(splits[6], 1), -480, 480).astype(jnp.int32),
        "obs_weight": jnp.clip(jnp.exp(math.log(16.0) - 2.7725887 * jax.random.uniform(splits[7], (QUANTITY_HEIGHTS, ROWS_F, COLS_F), jnp.float32) ** block_scale(splits[7], (QUANTITY_HEIGHTS, ROWS_F, COLS_F), ((2, 8),), -0.2, 0.2)), 1.0, 16.0),
    }


LON_RATE = 0.8
HIGH = lax.Precision.HIGHEST

def lon_table(col_count):
    across = jnp.arange(col_count)
    distance = across[None, :] - across[:, None]
    weight_scale = jnp.sqrt(jnp.float32(1.0 - LON_RATE * LON_RATE))
    powers = jnp.power(jnp.float32(LON_RATE), jnp.maximum(distance, 0).astype(jnp.float32))
    return jnp.where(distance >= 0, weight_scale * powers, jnp.float32(0.0))

def lon_interp(lon_weight, col_count):
    target = jnp.arange(lon_weight.shape[0])
    lower = target // 2
    higher = (lower + 1) % col_count
    fraction = lon_weight.astype(jnp.float32) / 256.0
    source = jnp.arange(col_count)[:, None]
    first_part = jnp.where(source == lower[None, :], fraction[None, :], jnp.float32(0.0))
    second_part = jnp.where(source == higher[None, :], 1.0 - fraction[None, :], jnp.float32(0.0))
    return first_part + second_part

def wind_terms(wind_east, wind_north):
    east_rate = wind_east.astype(jnp.float32) / 1024.0
    north_rate = wind_north.astype(jnp.float32) / 1024.0
    east_pos = jnp.maximum(east_rate, 0.0)
    east_neg = jnp.maximum(-east_rate, 0.0)
    north_pos = jnp.maximum(north_rate, 0.0)
    north_neg = jnp.maximum(-north_rate, 0.0)
    keep = 1.0 - east_pos - east_neg - north_pos - north_neg
    return (east_pos, east_neg, north_pos, north_neg, keep)

def advance(field_now, east_pos, east_neg, north_pos, north_neg, keep):
    padded = jnp.pad(field_now, ((0, 0), (1, 1), (0, 0)))
    result = keep * field_now + east_pos * jnp.roll(field_now, 1, axis=2)
    result = result + east_neg * jnp.roll(field_now, -1, axis=2)
    return result + north_pos * padded[:, :-2, :] + north_neg * padded[:, 2:, :]

def retreat(field_now, east_pos, east_neg, north_pos, north_neg, keep):
    from_south = jnp.pad(north_pos * field_now, ((0, 0), (0, 1), (0, 0)))[:, 1:, :]
    from_north = jnp.pad(north_neg * field_now, ((0, 0), (1, 0), (0, 0)))[:, :-1, :]
    result = keep * field_now + jnp.roll(east_pos * field_now, -1, axis=2)
    result = result + jnp.roll(east_neg * field_now, 1, axis=2)
    return result + from_south + from_north

def reference(perturbations, control, filter_rate, lat_weight, lon_weight, wind_east, wind_north, obs_weight):
    filter_table = lon_table(NC)
    interp = lon_interp(lon_weight, NC)
    shrink = jnp.sqrt(1.0 - filter_rate * filter_rate)
    spread = 1.0 / jnp.sqrt(jnp.float32(MEMBERS - 1))
    east_pos, east_neg, north_pos, north_neg, keep = wind_terms(wind_east, wind_north)

    def localize(member_field):
        smoothed = jnp.einsum('vrc,cd->vrd', member_field, filter_table, precision=HIGH)

        def forward_row(state_now, inputs):
            rate_row, shrink_row, row_vals = inputs
            state_now = rate_row[:, None] * state_now + shrink_row[:, None] * row_vals
            return (state_now, state_now)
        _, stacked = lax.scan(forward_row, jnp.zeros((QUANTITY_HEIGHTS, NC), jnp.float32), (filter_rate, shrink, jnp.moveaxis(smoothed, 1, 0)))
        return jnp.moveaxis(stacked, 0, 1)

    def accumulate(total_sum, member_pair):
        member_field, alpha_field = member_pair
        return (total_sum + member_field.astype(jnp.float32) * localize(alpha_field), None)
    summed_members, _ = lax.scan(accumulate, jnp.zeros((QUANTITY_HEIGHTS, LOWRES_LAT_TOTAL, NC), jnp.float32), (perturbations, control))
    increment = spread * summed_members
    upper = jnp.concatenate([increment[:, 1:, :], jnp.zeros((QUANTITY_HEIGHTS, 1, NC), jnp.float32)], axis=1)
    lat_frac = (lat_weight.astype(jnp.float32) / 256.0)[None, :, None]
    fine_rows = lat_frac * jnp.repeat(increment, 2, axis=1) + (1.0 - lat_frac) * jnp.repeat(upper, 2, axis=1)
    field_now = jnp.einsum('vrc,cd->vrd', fine_rows, interp, precision=HIGH)
    for step_index in range(STEPS):
        field_now = advance(field_now, east_pos, east_neg, north_pos, north_neg, keep)
    field_now = obs_weight * field_now
    for step_index in range(STEPS):
        field_now = retreat(field_now, east_pos, east_neg, north_pos, north_neg, keep)
    rows_adjoint = jnp.einsum('vrd,cd->vrc', field_now, interp, precision=HIGH)
    own_part = (lat_frac * rows_adjoint).reshape(QUANTITY_HEIGHTS, LOWRES_LAT_TOTAL, 2, NC).sum(axis=2)
    upper_part = ((1.0 - lat_frac) * rows_adjoint).reshape(QUANTITY_HEIGHTS, LOWRES_LAT_TOTAL, 2, NC).sum(axis=2)
    increment_adjoint = own_part + jnp.concatenate([jnp.zeros((QUANTITY_HEIGHTS, 1, NC), jnp.float32), upper_part[:, :-1, :]], axis=1)
    rates_next = jnp.concatenate([filter_rate[1:], jnp.zeros((1, QUANTITY_HEIGHTS), jnp.float32)], axis=0)

    def member_gradient(member_field):
        member_adjoint = spread * member_field.astype(jnp.float32) * increment_adjoint

        def backward_row(state_now, inputs):
            rate_next, row_vals = inputs
            state_now = row_vals + rate_next[:, None] * state_now
            return (state_now, state_now)
        _, stacked = lax.scan(backward_row, jnp.zeros((QUANTITY_HEIGHTS, NC), jnp.float32), (rates_next, jnp.moveaxis(member_adjoint, 1, 0)), reverse=True)
        scaled = jnp.moveaxis(stacked, 0, 1) * jnp.transpose(shrink)[:, :, None]
        return jnp.einsum('vrd,cd->vrc', scaled, filter_table, precision=HIGH)
    return control + lax.map(member_gradient, perturbations)
```

```python
import functools

import jax
import jax.numpy as jnp
import ml_dtypes
import numpy as np
from jax import lax
from jax.experimental import pallas as pl
from jax.experimental.pallas import tpu as pltpu
from jax.sharding import PartitionSpec as P

STEPS = 3
MESH = pl.DeviceIdType.MESH


LON_RATE = 0.8
HIGH = lax.Precision.HIGHEST


def with_halo(shard, sides, width):
    for axis, dim in sides:
        size, length = (lax.axis_size(axis), shard.shape[dim])
        up = [(i, (i + 1) % size) for i in range(size)]
        down = [(j, i) for i, j in up]
        last = lax.slice_in_dim(shard, length - width, length, axis=dim)
        leading = lax.slice_in_dim(shard, 0, width, axis=dim)
        before = lax.ppermute(last, axis, up)
        after = lax.ppermute(leading, axis, down)
        shard = jnp.concatenate([before, shard, after], axis=dim)
    return shard


def carried_in(part, axis, combine, identity, reverse):
    count = lax.axis_size(axis)
    place = lax.axis_index(axis)
    ahead = count - 1 - place if reverse else place
    gathered = jax.tree.map(lambda a: lax.all_gather(a, axis), part)
    state = jax.tree.map(lambda a, e: jnp.zeros_like(a) + jnp.asarray(e, a.dtype), part, identity)

    def one(turn, state):
        source = count - 1 - turn if reverse else turn
        return combine(
            state, jax.tree.map(lambda a: lax.dynamic_index_in_dim(a, source, 0, False), gathered)
        )

    return lax.fori_loop(0, ahead, one, state)


def shifted(block, axis, distance):
    devices = range(lax.axis_size(axis))
    route = [(i - distance, i) for i in devices if i - distance in devices]
    return lax.ppermute(block, axis, route)


def lon_table(col_count):
    across = jnp.arange(col_count)
    distance = across[None, :] - across[:, None]
    weight_scale = jnp.sqrt(jnp.float32(1.0 - LON_RATE * LON_RATE))
    powers = jnp.power(jnp.float32(LON_RATE), jnp.maximum(distance, 0).astype(jnp.float32))
    return jnp.where(distance >= 0, weight_scale * powers, jnp.float32(0.0))


def wind_terms(wind_east, wind_north):
    east_rate = wind_east.astype(jnp.float32) / 1024.0
    north_rate = wind_north.astype(jnp.float32) / 1024.0
    east_pos = jnp.maximum(east_rate, 0.0)
    east_neg = jnp.maximum(-east_rate, 0.0)
    north_pos = jnp.maximum(north_rate, 0.0)
    north_neg = jnp.maximum(-north_rate, 0.0)
    keep = 1.0 - east_pos - east_neg - north_pos - north_neg
    return (east_pos, east_neg, north_pos, north_neg, keep)


def compose(earlier, later):
    return (earlier[0] * later[0], later[0][None, :, None] * earlier[1] + later[1])


def advance(field_now, coeffs):
    east_pos, east_neg, north_pos, north_neg, keep = coeffs
    padded = with_halo(field_now, (("tile", 1),), 1)
    rows_pad = jnp.pad(field_now, ((0, 0), (0, 0), (1, 1)))
    result = keep * field_now + east_pos * padded[:, :-2, :] + east_neg * padded[:, 2:, :]
    return result + north_pos * rows_pad[:, :, :-2] + north_neg * rows_pad[:, :, 2:]


def retreat(field_now, coeffs):
    east_pos, east_neg, north_pos, north_neg, keep = coeffs
    padded = with_halo(field_now, (("tile", 1),), 1)
    from_east = east_pos[2:, :] * padded[:, 2:, :]
    from_west = east_neg[:-2, :] * padded[:, :-2, :]
    from_south = jnp.pad(north_pos[1:-1, :] * field_now, ((0, 0), (0, 0), (0, 1)))[:, :, 1:]
    from_north = jnp.pad(north_neg[1:-1, :] * field_now, ((0, 0), (0, 0), (1, 0)))[:, :, :-1]
    return keep[1:-1, :] * field_now + from_east + from_west + from_south + from_north


def local(
    perturbations, control, filter_rate, lat_weight, lon_weight, wind_east, wind_north, obs_weight
):
    member_count, level_count, coarse_rows, col_count = control.shape
    filter_table = lon_table(col_count)
    shrink = jnp.sqrt(1.0 - filter_rate * filter_rate)
    spread = 1.0 / jnp.sqrt(jnp.float32(member_count * lax.axis_size("mem") - 1))
    start_pair = (
        jnp.ones((level_count,), jnp.float32),
        jnp.zeros((member_count, level_count, col_count), jnp.float32),
    )
    smoothed = jnp.einsum("mvrc,cd->rmvd", control, filter_table, precision=HIGH)

    def forward_row(pair_now, inputs):
        gain_now, stretch = pair_now
        rate_row, shrink_row, row_vals = inputs
        gain_now = rate_row * gain_now
        stretch = rate_row[None, :, None] * stretch + shrink_row[None, :, None] * row_vals
        return ((gain_now, stretch), (gain_now, stretch))

    summary, (gains, stretches) = lax.scan(forward_row, start_pair, (filter_rate, shrink, smoothed))
    _, incoming = carried_in(summary, "tile", compose, start_pair, False)
    localized = gains[:, None, :, None] * incoming[None] + stretches
    partial_sum = spread * jnp.einsum(
        "mvrc,rmvc->vrc", perturbations.astype(jnp.float32), localized, precision=HIGH
    )
    increment = lax.psum(partial_sum, "mem")
    weight_here = obs_weight
    weight_here = jnp.swapaxes(weight_here, 1, 2)
    winds_turned = jnp.stack([jnp.transpose(wind_east), jnp.transpose(wind_north)])
    wind_halo = with_halo(winds_turned, (("tile", 1),), 1)
    halo_coeffs = wind_terms(wind_halo[0], wind_halo[1])
    inner_coeffs = tuple((term_item[1:-1, :] for term_item in halo_coeffs))
    level_here = increment.shape[0]
    tile_count = lax.axis_size("tile")
    band_cols = wind_east.shape[1]
    next_first = shifted(increment[:, :1, :], "tile", -1)
    window = band_cols // 2 + 2
    starts = jnp.arange(tile_count) * band_cols // 2
    cols_index = (starts[:, None] + jnp.arange(window)[None, :]) % col_count
    select = (jnp.arange(col_count)[:, None, None] == cols_index[None]).astype(jnp.float32)
    extended = jnp.concatenate([increment, next_first], axis=1)
    windows = jnp.einsum("vrc,cnk->vnrk", extended, select, precision=HIGH)
    arrived = lax.all_to_all(windows, "tile", split_axis=1, concat_axis=1, tiled=True)
    lat_every = lax.all_gather(lat_weight, "tile", axis=0, tiled=True)
    frac_every = (lat_every.astype(jnp.float32) / 256.0).reshape(1, tile_count, 2 * coarse_rows, 1)
    lower_rows = jnp.repeat(arrived[:, :, :-1, :], 2, axis=2)
    higher_rows = jnp.repeat(arrived[:, :, 1:, :], 2, axis=2)
    fine_window = (frac_every * lower_rows + (1.0 - frac_every) * higher_rows).reshape(
        level_here, tile_count * 2 * coarse_rows, window
    )
    first_col = lax.axis_index("tile") * band_cols
    fractions = (
        lax.dynamic_slice_in_dim(lon_weight, first_col, band_cols, 0).astype(jnp.float32) / 256.0
    )
    lower_local = (first_col + jnp.arange(band_cols)) // 2 - first_col // 2
    slots = jnp.arange(window)[:, None]
    band_interp = jnp.where(
        slots == lower_local[None, :], fractions[None, :], jnp.float32(0.0)
    ) + jnp.where(slots == lower_local[None, :] + 1, 1.0 - fractions[None, :], jnp.float32(0.0))
    field_now = jnp.einsum("vqk,kj->vjq", fine_window, band_interp, precision=HIGH)
    for step_index in range(STEPS):
        field_now = advance(field_now, inner_coeffs)
    field_now = weight_here * field_now
    for step_index in range(STEPS):
        field_now = retreat(field_now, halo_coeffs)
    rows_window = jnp.einsum("vjq,kj->vqk", field_now, band_interp, precision=HIGH).reshape(
        level_here, tile_count, 2 * coarse_rows, window
    )
    own_window = (
        (frac_every * rows_window)
        .reshape(level_here, tile_count, coarse_rows, 2, window)
        .sum(axis=3)
    )
    above_window = (
        ((1.0 - frac_every) * rows_window)
        .reshape(level_here, tile_count, coarse_rows, 2, window)
        .sum(axis=3)
    )
    extended_adjoint = jnp.pad(own_window, ((0, 0), (0, 0), (0, 1), (0, 0))) + jnp.pad(
        above_window, ((0, 0), (0, 0), (1, 0), (0, 0))
    )
    returned = lax.all_to_all(extended_adjoint, "tile", split_axis=1, concat_axis=1, tiled=True)
    column_sums = jnp.einsum("vnrk,cnk->vrc", returned, select, precision=HIGH)
    base_part = column_sums[:, :coarse_rows, :]
    edge_row = column_sums[:, coarse_rows:, :]
    carried = shifted(edge_row, "tile", 1)
    increment_adjoint = base_part + jnp.concatenate(
        [carried, jnp.zeros((level_here, coarse_rows - 1, col_count), jnp.float32)], axis=1
    )
    member_adjoint = spread * jnp.einsum(
        "mvrc,vrc->rmvc", perturbations.astype(jnp.float32), increment_adjoint, precision=HIGH
    )

    def backward_row(pair_now, inputs):
        gain_now, stretch = pair_now
        rate_row, row_vals = inputs
        outputs_here = (gain_now, stretch)
        gain_now = rate_row * gain_now
        stretch = rate_row[None, :, None] * (row_vals + stretch)
        return ((gain_now, stretch), outputs_here)

    summary_up, (gains_up, stretches_up) = lax.scan(
        backward_row, start_pair, (filter_rate, member_adjoint), reverse=True
    )
    _, incoming_up = carried_in(summary_up, "tile", compose, start_pair, True)
    summed = member_adjoint + gains_up[:, None, :, None] * incoming_up[None] + stretches_up
    scaled = summed * shrink[:, None, :, None]
    return control + jnp.einsum("rmvd,cd->mvrc", scaled, filter_table, precision=HIGH)

def split(x):
    high = x.astype(jnp.bfloat16)
    return high, (x - high.astype(jnp.float32)).astype(jnp.bfloat16)


def product(a, b, turned):
    dims = (((1,), (1 if turned else 0,)), ((), ()))

    def one(left, right):
        return lax.dot_general(left, right, dims, preferred_element_type=jnp.float32)

    total = None
    for i, left in enumerate(a):
        for j, right in enumerate(b):
            if i + j < 2:
                term = one(left, right)
                total = term if total is None else total + term
    return total


def hessian_kernel(
    tiles, mems, rows_fine, spread,
    ctl, prt, rates, small, winds, obs, lon, table_high, table_low,
    out,
    smalls, winds_all, obs_all, send_a, got_a, send_b, got_b, parts, parts_got,
    levels_out, levels_in, adj_out, adj_in, own_adj, adj_all, send_c, got_c, send_d, got_d,
    tile_send, tile_recv, mem_send, mem_recv,
):
    rows, members, levels, cols = ctl.shape
    t = lax.axis_index("tile")
    m = lax.axis_index("mem")
    f32 = jnp.float32
    started = []

    barrier = pltpu.get_barrier_semaphore()
    for d in range(1, tiles):
        pl.semaphore_signal(
            barrier, inc=1, device_id={"tile": lax.rem(t + d, tiles)}, device_id_type=MESH
        )
    for d in range(1, mems):
        pl.semaphore_signal(
            barrier, inc=1, device_id={"mem": lax.rem(m + d, mems)}, device_id_type=MESH
        )

    def spread_out(kind, axis, source, target):
        size, me = (tiles, t) if axis == "tile" else (mems, m)
        sends, recvs = (tile_send, tile_recv) if axis == "tile" else (mem_send, mem_recv)
        copies = []
        for d in range(1, size):
            dest = lax.rem(me + d, size)
            copy = pltpu.make_async_remote_copy(
                src_ref=source(dest),
                dst_ref=target.at[me],
                send_sem=sends.at[kind, d],
                recv_sem=recvs.at[kind, d],
                device_id={axis: dest},
                device_id_type=MESH,
            )
            copy.start()
            copies.append(copy)
        target[me] = source(me)[...]
        started.extend(copies)
        return copies

    def arrive(copies):
        for copy in copies:
            copy.wait_recv()

    rate = [rates[:, r : r + 1] for r in range(rows)]
    shrink = [jnp.sqrt(1.0 - a * a) for a in rate]

    def store_pieces(target, value):
        for lane_part in range(-(-cols // 128)):
            low = 128 * lane_part
            width = min(128, cols - low)
            for group in range(levels // 8):
                piece = lane_part * (levels // 8) + group
                block = value[:, 8 * group : 8 * group + 8, low : low + width]
                if width < 128:
                    block = jnp.concatenate(
                        [block, jnp.zeros((members, 8, 128 - width), f32)], axis=2
                    )
                target[piece] = block

    def load_pieces(source):
        groups = levels // 8
        lanes = []
        for lane_part in range(-(-cols // 128)):
            width = min(128, cols - 128 * lane_part)
            blocks = [source[lane_part * groups + g] for g in range(groups)]
            lanes.append(jnp.concatenate(blocks, axis=1)[:, :, :width])
        return jnp.concatenate(lanes, axis=2)

    local_rows = []
    state = None
    for r in range(rows):
        term = shrink[r] * ctl[r]
        state = term if r == 0 else rate[r] * state + term
        local_rows.append(state)
    store_pieces(send_a, state)

    pl.semaphore_wait(barrier, tiles - 1 + mems - 1)
    small_copies = spread_out(0, "tile", lambda dest: small, smalls)
    carry_copies = spread_out(1, "tile", lambda dest: send_a.at[dest], got_a)
    wind_copies = spread_out(2, "tile", lambda dest: winds, winds_all)
    obs_copies = spread_out(3, "tile", lambda dest: obs.at[dest], obs_all)

    table = (table_high[...], table_low[...])

    def smooth(x, turned):
        flat = x.reshape(members * levels, cols)
        return product(split(flat), table, turned).reshape(members, levels, cols)

    smooth_rows = [smooth(x, False) for x in local_rows]

    arrive(small_copies)
    group = lax.rem(t, levels // 8)
    lane = lax.broadcasted_iota(jnp.int32, (8, 128), 1)
    sub = lax.broadcasted_iota(jnp.int32, (8, 128), 0)
    gain_mask = lane == sub + 8 * group
    gains = []
    for s in range(tiles):
        row = smalls[s, 1:2, :]
        gains.append(jnp.sum(jnp.where(gain_mask, row, 0.0), axis=1, keepdims=True))
    arrive(carry_copies)
    state = jnp.zeros((members, 8, 128), f32)
    for s in range(tiles):
        send_b[s] = state
        state = gains[s] * state + got_a[s]
    back_copies = spread_out(4, "tile", lambda dest: send_b.at[dest], got_b)

    levels_out[...] = jnp.zeros_like(levels_out)
    interp_row = lax.broadcasted_iota(jnp.int32, (lon.shape[0], cols), 0) // 2
    interp_col = lax.broadcasted_iota(jnp.int32, (lon.shape[0], cols), 1)
    west = lon[...]
    interp = jnp.where(interp_col == interp_row, west, 0.0) + jnp.where(
        interp_col == lax.rem(interp_row + 1, cols), 1.0 - west, 0.0
    )
    interp = (interp.astype(jnp.bfloat16),)
    lat = smalls[0, 0:1, :]
    for s in range(1, tiles):
        lat = lat + smalls[s, 0:1, :]
    slot = lax.broadcasted_iota(jnp.int32, (8 * tiles, 128), 0)
    fine_row = lax.broadcasted_iota(jnp.int32, (8 * tiles, 128), 1) // 2
    coarse = jnp.where(slot % 8 < rows, slot // 8 * rows + slot % 8, -2)
    inside = fine_row < rows * tiles
    lat_table = jnp.where((fine_row == coarse) & inside, lat, 0.0) + jnp.where(
        (fine_row + 1 == coarse) & inside, 1.0 - lat, 0.0
    )
    lat_table = (lat_table.astype(jnp.bfloat16),)

    arrive(back_copies)
    carried = smooth(load_pieces(got_b), False)
    gain = None
    group_levels = levels // mems
    for r in range(rows):
        gain = rate[r] if r == 0 else gain * rate[r]
        localized = gain * carried + smooth_rows[r]
        partial = spread * jnp.sum(prt[r] * localized, axis=0)
        for i in range(mems):
            parts[i, r] = partial[i * group_levels : (i + 1) * group_levels]
    part_copies = spread_out(0, "mem", lambda dest: parts.at[dest], parts_got)

    arrive(wind_copies)
    arrive(obs_copies)
    count = lon.shape[0]
    both = winds_all[...].reshape(count, 128)
    keep_lane = lax.broadcasted_iota(jnp.int32, (count, 128), 1) < rows_fine
    east = jnp.where(keep_lane, both, 0.0)
    north = jnp.where(keep_lane, pltpu.roll(both, 64, 1), 0.0)
    east_pos = jnp.maximum(east, 0.0)
    east_neg = jnp.maximum(-east, 0.0)
    north_pos = jnp.maximum(north, 0.0)
    north_neg = jnp.maximum(-north, 0.0)
    keep = 1.0 - east_pos - east_neg - north_pos - north_neg
    arrive(part_copies)
    for r in range(rows):
        total = parts_got[0, r]
        for i in range(1, mems):
            total = total + parts_got[i, r]
        for level in range(group_levels):
            levels_out[level, r : r + 1, :] = total[level : level + 1, :]
    level_copies = spread_out(5, "tile", lambda dest: levels_out.at[dest], levels_in)
    arrive(level_copies)

    increment = levels_in[...].reshape(8 * tiles, cols)
    by_lon = product(interp, split(increment), True)
    g = product(split(by_lon), lat_table, False)
    for _ in range(STEPS):
        g = (
            keep * g
            + east_pos * pltpu.roll(g, 1, 0)
            + east_neg * pltpu.roll(g, count - 1, 0)
            + north_pos * pltpu.roll(g, 1, 1)
            + north_neg * pltpu.roll(g, 127, 1)
        )
    g = obs_all[...].reshape(count, 128) * g
    for _ in range(STEPS):
        g = (
            keep * g
            + pltpu.roll(east_pos * g, count - 1, 0)
            + pltpu.roll(east_neg * g, 1, 0)
            + pltpu.roll(north_pos * g, 127, 1)
            + pltpu.roll(north_neg * g, 1, 1)
        )
    by_lat = product(lat_table, split(g), True)
    adjoint = product(split(by_lat), interp, False)
    adj_out[...] = adjoint.reshape(tiles, 8, cols)
    adj_copies = spread_out(6, "tile", lambda dest: adj_out.at[dest], adj_in)
    arrive(adj_copies)
    for r in range(rows):
        for level in range(group_levels):
            own_adj[r, level : level + 1, :] = adj_in[level, r : r + 1, :]
    own_copies = spread_out(1, "mem", lambda dest: own_adj, adj_all)
    arrive(own_copies)

    member_rows = []
    for r in range(rows):
        field = jnp.concatenate([adj_all[i, r] for i in range(mems)], axis=0)
        member_rows.append((spread * field) * prt[r])
    state = member_rows[rows - 1]
    summed = [state]
    for r in reversed(range(rows - 1)):
        state = member_rows[r] + rate[r + 1] * state
        summed.insert(0, state)
    store_pieces(send_c, rate[0] * state)
    up_copies = spread_out(7, "tile", lambda dest: send_c.at[dest], got_c)
    smooth_rows = [smooth(shrink[r] * summed[r], True) for r in range(rows)]
    arrive(up_copies)
    state = jnp.zeros((members, 8, 128), f32)
    for s in reversed(range(tiles)):
        send_d[s] = state
        state = gains[s] * state + got_c[s]
    last_copies = spread_out(8, "tile", lambda dest: send_d.at[dest], got_d)
    arrive(last_copies)
    carried = smooth(load_pieces(got_d), True)
    gain = None
    for r in reversed(range(rows)):
        gain = jnp.ones_like(rate[r]) if r == rows - 1 else gain * rate[r + 1]
        out[r] = ctl[r] + smooth_rows[r] + (shrink[r] * gain) * carried
    for copy in started:
        copy.wait_send()


def fused(
    perturbations, control, filter_rate, lat_weight, lon_weight, wind_east, wind_north, obs_weight
):
    members, levels, rows, cols = control.shape
    tiles, mems = lax.axis_size("tile"), lax.axis_size("mem")
    t, m = lax.axis_index("tile"), lax.axis_index("mem")
    f32 = jnp.float32
    rows_fine, band = wind_east.shape
    ctl = jnp.transpose(control, (2, 0, 1, 3))
    prt = jnp.transpose(perturbations, (2, 0, 1, 3)).astype(f32)
    lat_lane = jnp.arange(128)[None, :] - t * lat_weight.shape[0]
    lat_slot = jnp.arange(lat_weight.shape[0])[:, None]
    lat_row = jnp.sum(
        jnp.where(lat_lane == lat_slot, lat_weight.astype(f32)[:, None] / 256.0, 0.0), axis=0
    )
    gain_row = jnp.pad(jnp.prod(filter_rate, axis=0), (0, 128 - levels))
    small = jnp.concatenate([lat_row[None], gain_row[None], jnp.zeros((6, 128), f32)], axis=0)
    winds = jnp.concatenate(
        [
            jnp.pad(jnp.transpose(w).astype(f32) / 1024.0, ((0, 0), (0, 64 - rows_fine)))
            for w in (wind_east, wind_north)
        ],
        axis=1,
    )
    group = levels // mems
    obs = lax.dynamic_slice_in_dim(obs_weight, m * group, group, 0)
    obs = jnp.pad(jnp.swapaxes(obs, 1, 2), ((0, 0), (0, 0), (0, 128 - rows_fine)))
    lon = lon_weight.astype(f32)[:, None] / 256.0
    across = np.arange(cols)
    distance = across[None, :] - across[:, None]
    full = np.where(
        distance >= 0, np.sqrt(1.0 - LON_RATE**2) * LON_RATE ** np.maximum(distance, 0.0), 0.0
    ).astype(np.float32)
    table_high = full.astype(ml_dtypes.bfloat16)
    table_low = (full - table_high.astype(np.float32)).astype(ml_dtypes.bfloat16)
    spread = float(1.0 / np.sqrt(np.float32(members * mems - 1)))
    piece = (tiles, members, 8, 128)
    vmem = pl.BlockSpec(memory_space=pltpu.VMEM)
    result = pl.pallas_call(
        functools.partial(hessian_kernel, tiles, mems, rows_fine, spread),
        out_shape=jax.ShapeDtypeStruct(ctl.shape, f32),
        in_specs=[vmem] * 9,
        out_specs=vmem,
        scratch_shapes=[
            pltpu.VMEM((tiles, 8, 128), f32),
            pltpu.VMEM((tiles, band, 128), f32),
            pltpu.VMEM((tiles, band, 128), f32),
            *[pltpu.VMEM(piece, f32)] * 4,
            *[pltpu.VMEM((mems, rows, group, cols), f32)] * 2,
            *[pltpu.VMEM((tiles, 8, cols), f32)] * 4,
            pltpu.VMEM((rows, group, cols), f32),
            pltpu.VMEM((mems, rows, group, cols), f32),
            *[pltpu.VMEM(piece, f32)] * 4,
            pltpu.SemaphoreType.DMA((9, tiles)),
            pltpu.SemaphoreType.DMA((9, tiles)),
            pltpu.SemaphoreType.DMA((2, mems)),
            pltpu.SemaphoreType.DMA((2, mems)),
        ],
        compiler_params=pltpu.CompilerParams(
            collective_id=0, has_side_effects=True, vmem_limit_bytes=40 * 2**20
        ),
    )(ctl, prt, filter_rate.T, small, winds, obs, lon, table_high, table_low)
    return jnp.transpose(result, (1, 2, 0, 3))


def plan(
    perturbations, control, filter_rate, lat_weight, lon_weight, wind_east, wind_north, obs_weight
):
    levels, rows, cols = control.shape[1:]
    tiles, mems = lax.axis_size("tile"), lax.axis_size("mem")
    fits = (
        levels == tiles * mems
        and tiles == 8
        and levels // 8 * -(-cols // 128) == tiles
        and rows <= 8
        and wind_east.shape[0] <= 64
        and wind_east.shape[1] % 8 == 0
        and levels <= 128
    )
    return (fused if fits else local)(
        perturbations, control, filter_rate, lat_weight, lon_weight, wind_east, wind_north,
        obs_weight,
    )


def solution(mesh):
    placed = (
        P("mem", None, "tile", None),
        P("mem", None, "tile", None),
        P("tile", None),
        P("tile"),
        P(),
        P(None, "tile"),
        P(None, "tile"),
        P(None, None, "tile"),
    )
    return jax.shard_map(
        plan, mesh=mesh, in_specs=placed, out_specs=P("mem", None, "tile", None), check_vma=False
    )
```

```python
import functools
import math

import jax
import jax.numpy as jnp
import numpy as np
from jax import lax
from jax.experimental import pallas as pl
from jax.experimental.pallas import tpu as pltpu
from jax.sharding import PartitionSpec as P

STEPS = 3
MESH = pl.DeviceIdType.MESH


LON_RATE = 0.8
HIGH = lax.Precision.HIGHEST


def with_halo(shard, sides, width):
    for axis, dim in sides:
        size, length = (lax.axis_size(axis), shard.shape[dim])
        up = [(i, (i + 1) % size) for i in range(size)]
        down = [(j, i) for i, j in up]
        last = lax.slice_in_dim(shard, length - width, length, axis=dim)
        leading = lax.slice_in_dim(shard, 0, width, axis=dim)
        before = lax.ppermute(last, axis, up)
        after = lax.ppermute(leading, axis, down)
        shard = jnp.concatenate([before, shard, after], axis=dim)
    return shard


def carried_in(part, axis, combine, identity, reverse):
    count = lax.axis_size(axis)
    place = lax.axis_index(axis)
    ahead = count - 1 - place if reverse else place
    gathered = jax.tree.map(lambda a: lax.all_gather(a, axis), part)
    state = jax.tree.map(lambda a, e: jnp.zeros_like(a) + jnp.asarray(e, a.dtype), part, identity)

    def one(turn, state):
        source = count - 1 - turn if reverse else turn
        return combine(
            state, jax.tree.map(lambda a: lax.dynamic_index_in_dim(a, source, 0, False), gathered)
        )

    return lax.fori_loop(0, ahead, one, state)


def shifted(block, axis, distance):
    devices = range(lax.axis_size(axis))
    route = [(i - distance, i) for i in devices if i - distance in devices]
    return lax.ppermute(block, axis, route)


def lon_table(col_count):
    across = jnp.arange(col_count)
    distance = across[None, :] - across[:, None]
    weight_scale = jnp.sqrt(jnp.float32(1.0 - LON_RATE * LON_RATE))
    powers = jnp.power(jnp.float32(LON_RATE), jnp.maximum(distance, 0).astype(jnp.float32))
    return jnp.where(distance >= 0, weight_scale * powers, jnp.float32(0.0))


def wind_terms(wind_east, wind_north):
    east_rate = wind_east.astype(jnp.float32) / 1024.0
    north_rate = wind_north.astype(jnp.float32) / 1024.0
    east_pos = jnp.maximum(east_rate, 0.0)
    east_neg = jnp.maximum(-east_rate, 0.0)
    north_pos = jnp.maximum(north_rate, 0.0)
    north_neg = jnp.maximum(-north_rate, 0.0)
    keep = 1.0 - east_pos - east_neg - north_pos - north_neg
    return (east_pos, east_neg, north_pos, north_neg, keep)


def compose(earlier, later):
    return (earlier[0] * later[0], later[0][None, :, None] * earlier[1] + later[1])


def advance(field_now, coeffs):
    east_pos, east_neg, north_pos, north_neg, keep = coeffs
    padded = with_halo(field_now, (("tile", 1),), 1)
    rows_pad = jnp.pad(field_now, ((0, 0), (0, 0), (1, 1)))
    result = keep * field_now + east_pos * padded[:, :-2, :] + east_neg * padded[:, 2:, :]
    return result + north_pos * rows_pad[:, :, :-2] + north_neg * rows_pad[:, :, 2:]


def retreat(field_now, coeffs):
    east_pos, east_neg, north_pos, north_neg, keep = coeffs
    padded = with_halo(field_now, (("tile", 1),), 1)
    from_east = east_pos[2:, :] * padded[:, 2:, :]
    from_west = east_neg[:-2, :] * padded[:, :-2, :]
    from_south = jnp.pad(north_pos[1:-1, :] * field_now, ((0, 0), (0, 0), (0, 1)))[:, :, 1:]
    from_north = jnp.pad(north_neg[1:-1, :] * field_now, ((0, 0), (0, 0), (1, 0)))[:, :, :-1]
    return keep[1:-1, :] * field_now + from_east + from_west + from_south + from_north


def local(
    perturbations, control, filter_rate, lat_weight, lon_weight, wind_east, wind_north, obs_weight
):
    member_count, level_count, coarse_rows, col_count = control.shape
    filter_table = lon_table(col_count)
    shrink = jnp.sqrt(1.0 - filter_rate * filter_rate)
    spread = 1.0 / jnp.sqrt(jnp.float32(member_count * lax.axis_size("mem") - 1))
    start_pair = (
        jnp.ones((level_count,), jnp.float32),
        jnp.zeros((member_count, level_count, col_count), jnp.float32),
    )
    smoothed = jnp.einsum("mvrc,cd->rmvd", control, filter_table, precision=HIGH)

    def forward_row(pair_now, inputs):
        gain_now, stretch = pair_now
        rate_row, shrink_row, row_vals = inputs
        gain_now = rate_row * gain_now
        stretch = rate_row[None, :, None] * stretch + shrink_row[None, :, None] * row_vals
        return ((gain_now, stretch), (gain_now, stretch))

    summary, (gains, stretches) = lax.scan(forward_row, start_pair, (filter_rate, shrink, smoothed))
    _, incoming = carried_in(summary, "tile", compose, start_pair, False)
    localized = gains[:, None, :, None] * incoming[None] + stretches
    partial_sum = spread * jnp.einsum(
        "mvrc,rmvc->vrc", perturbations.astype(jnp.float32), localized, precision=HIGH
    )
    increment = lax.psum(partial_sum, "mem")
    weight_here = obs_weight
    weight_here = jnp.swapaxes(weight_here, 1, 2)
    winds_turned = jnp.stack([jnp.transpose(wind_east), jnp.transpose(wind_north)])
    wind_halo = with_halo(winds_turned, (("tile", 1),), 1)
    halo_coeffs = wind_terms(wind_halo[0], wind_halo[1])
    inner_coeffs = tuple((term_item[1:-1, :] for term_item in halo_coeffs))
    level_here = increment.shape[0]
    tile_count = lax.axis_size("tile")
    band_cols = wind_east.shape[1]
    next_first = shifted(increment[:, :1, :], "tile", -1)
    window = band_cols // 2 + 2
    starts = jnp.arange(tile_count) * band_cols // 2
    cols_index = (starts[:, None] + jnp.arange(window)[None, :]) % col_count
    select = (jnp.arange(col_count)[:, None, None] == cols_index[None]).astype(jnp.float32)
    extended = jnp.concatenate([increment, next_first], axis=1)
    windows = jnp.einsum("vrc,cnk->vnrk", extended, select, precision=HIGH)
    arrived = lax.all_to_all(windows, "tile", split_axis=1, concat_axis=1, tiled=True)
    lat_every = lax.all_gather(lat_weight, "tile", axis=0, tiled=True)
    frac_every = (lat_every.astype(jnp.float32) / 256.0).reshape(1, tile_count, 2 * coarse_rows, 1)
    lower_rows = jnp.repeat(arrived[:, :, :-1, :], 2, axis=2)
    higher_rows = jnp.repeat(arrived[:, :, 1:, :], 2, axis=2)
    fine_window = (frac_every * lower_rows + (1.0 - frac_every) * higher_rows).reshape(
        level_here, tile_count * 2 * coarse_rows, window
    )
    first_col = lax.axis_index("tile") * band_cols
    fractions = (
        lax.dynamic_slice_in_dim(lon_weight, first_col, band_cols, 0).astype(jnp.float32) / 256.0
    )
    lower_local = (first_col + jnp.arange(band_cols)) // 2 - first_col // 2
    slots = jnp.arange(window)[:, None]
    band_interp = jnp.where(
        slots == lower_local[None, :], fractions[None, :], jnp.float32(0.0)
    ) + jnp.where(slots == lower_local[None, :] + 1, 1.0 - fractions[None, :], jnp.float32(0.0))
    field_now = jnp.einsum("vqk,kj->vjq", fine_window, band_interp, precision=HIGH)
    for step_index in range(STEPS):
        field_now = advance(field_now, inner_coeffs)
    field_now = weight_here * field_now
    for step_index in range(STEPS):
        field_now = retreat(field_now, halo_coeffs)
    rows_window = jnp.einsum("vjq,kj->vqk", field_now, band_interp, precision=HIGH).reshape(
        level_here, tile_count, 2 * coarse_rows, window
    )
    own_window = (
        (frac_every * rows_window)
        .reshape(level_here, tile_count, coarse_rows, 2, window)
        .sum(axis=3)
    )
    above_window = (
        ((1.0 - frac_every) * rows_window)
        .reshape(level_here, tile_count, coarse_rows, 2, window)
        .sum(axis=3)
    )
    extended_adjoint = jnp.pad(own_window, ((0, 0), (0, 0), (0, 1), (0, 0))) + jnp.pad(
        above_window, ((0, 0), (0, 0), (1, 0), (0, 0))
    )
    returned = lax.all_to_all(extended_adjoint, "tile", split_axis=1, concat_axis=1, tiled=True)
    column_sums = jnp.einsum("vnrk,cnk->vrc", returned, select, precision=HIGH)
    base_part = column_sums[:, :coarse_rows, :]
    edge_row = column_sums[:, coarse_rows:, :]
    carried = shifted(edge_row, "tile", 1)
    increment_adjoint = base_part + jnp.concatenate(
        [carried, jnp.zeros((level_here, coarse_rows - 1, col_count), jnp.float32)], axis=1
    )
    member_adjoint = spread * jnp.einsum(
        "mvrc,vrc->rmvc", perturbations.astype(jnp.float32), increment_adjoint, precision=HIGH
    )

    def backward_row(pair_now, inputs):
        gain_now, stretch = pair_now
        rate_row, row_vals = inputs
        outputs_here = (gain_now, stretch)
        gain_now = rate_row * gain_now
        stretch = rate_row[None, :, None] * (row_vals + stretch)
        return ((gain_now, stretch), outputs_here)

    summary_up, (gains_up, stretches_up) = lax.scan(
        backward_row, start_pair, (filter_rate, member_adjoint), reverse=True
    )
    _, incoming_up = carried_in(summary_up, "tile", compose, start_pair, True)
    summed = member_adjoint + gains_up[:, None, :, None] * incoming_up[None] + stretches_up
    scaled = summed * shrink[:, None, :, None]
    return control + jnp.einsum("rmvd,cd->mvrc", scaled, filter_table, precision=HIGH)

def split(x):
    high = x.astype(jnp.bfloat16)
    return high, (x - high.astype(jnp.float32)).astype(jnp.bfloat16)


def product(a, b, turned):
    dims = (((1,), (1 if turned else 0,)), ((), ()))

    def one(left, right):
        return lax.dot_general(left, right, dims, preferred_element_type=jnp.float32)

    total = None
    for i, left in enumerate(a):
        for j, right in enumerate(b):
            if i + j < 2:
                term = one(left, right)
                total = term if total is None else total + term
    return total


def expand(ref, count):
    return jnp.concatenate(
        [jnp.broadcast_to(ref[q : q + 1, :], (8, 128))[None] for q in range(count)], axis=0
    )


def wide(x):
    pad = jnp.zeros(x.shape[:-1] + (128 - x.shape[-1],), x.dtype)
    return jnp.concatenate([x, pad], axis=x.ndim - 1)


def placed_at(x, source, target, width):
    moved = pltpu.roll(x, (target - source) % 128, 1)
    lane = lax.broadcasted_iota(jnp.int32, x.shape, 1)
    return jnp.where((lane >= target) & (lane < target + width), moved, 0.0)


def column(row):
    count = row.shape[1]
    sub = lax.broadcasted_iota(jnp.int32, (count, count), 0)
    lane = lax.broadcasted_iota(jnp.int32, (count, count), 1)
    return jnp.sum(jnp.where(sub == lane, row, 0.0), axis=1, keepdims=True)


def hessian_kernel(
    tiles, mems, spread,
    ctl_hbm, prt_hbm, rates_hbm, lat_hbm, lon_hbm, east_hbm, north_hbm, obs_hbm,
    out,
    ctl, prt, rates, lat_in, lon_in, east_in, north_in, obs_in,
    small, smalls, halo_out, halo_in, wind_rows, weights, send_a, got_a, send_b, got_b,
    parts, parts_got, rows_out, rows_in, adj_out, adj_in, own_adj, adj_all,
    send_c, got_c, send_d, got_d, interp,
    local_sem, halo_send, halo_recv, tile_send, tile_recv, mem_send, mem_recv,
):
    members, rows, levels, cols = ctl.shape
    t = lax.axis_index("tile")
    m = lax.axis_index("mem")
    f32 = jnp.float32
    started = []
    group_levels = levels // mems
    rows_fine, band = east_in.shape
    halo = 2 * STEPS
    width = band + 2 * halo

    loads = []
    sources = (
        (rates_hbm, rates), (ctl_hbm, ctl), (lat_hbm, lat_in), (east_hbm, east_in),
        (north_hbm, north_in), (obs_hbm.at[pl.ds(m * group_levels, group_levels)], obs_in),
        (lon_hbm, lon_in), (prt_hbm, prt),
    )
    for i, (source, target) in enumerate(sources):
        load = pltpu.make_async_copy(source, target, local_sem.at[i])
        load.start()
        loads.append(load)

    barrier = pltpu.get_barrier_semaphore()
    for d in range(1, tiles):
        pl.semaphore_signal(
            barrier, inc=1, device_id={"tile": lax.rem(t + d, tiles)}, device_id_type=MESH
        )
    for d in range(1, mems):
        pl.semaphore_signal(
            barrier, inc=1, device_id={"mem": lax.rem(m + d, mems)}, device_id_type=MESH
        )

    def spread_out(kind, axis, source, target):
        size, me = (tiles, t) if axis == "tile" else (mems, m)
        sends, recvs = (tile_send, tile_recv) if axis == "tile" else (mem_send, mem_recv)
        copies = []
        for d in range(1, size):
            dest = lax.rem(me + d, size)
            copy = pltpu.make_async_remote_copy(
                src_ref=source(dest),
                dst_ref=target.at[me],
                send_sem=sends.at[kind, d],
                recv_sem=recvs.at[kind, d],
                device_id={axis: dest},
                device_id_type=MESH,
            )
            copy.start()
            copies.append(copy)
        target[me] = source(me)[...]
        started.extend(copies)
        return copies

    def arrive(copies):
        for copy in copies:
            copy.wait_recv()

    def store_pieces(target, value):
        for lane_part in range(-(-cols // 128)):
            low = 128 * lane_part
            span = min(128, cols - low)
            for group in range(levels // 8):
                piece = lane_part * (levels // 8) + group
                block = value[:, 8 * group : 8 * group + 8, low : low + span]
                target[piece] = wide(block) if span < 128 else block

    def load_pieces(source):
        groups = levels // 8
        lanes = []
        for lane_part in range(-(-cols // 128)):
            span = min(128, cols - 128 * lane_part)
            blocks = [source[lane_part * groups + g] for g in range(groups)]
            lanes.append(jnp.concatenate(blocks, axis=1)[:, :, :span])
        return jnp.concatenate(lanes, axis=2)

    loads[0].wait()
    rate = [column(rates[r : r + 1, :]) for r in range(rows)]
    shrink = [jnp.sqrt(1.0 - a * a) for a in rate]
    gain_row = rates[0:1, :]
    for r in range(1, rows):
        gain_row = gain_row * rates[r : r + 1, :]
    loads[1].wait()
    local_rows = []
    state = None
    for r in range(rows):
        term = shrink[r] * ctl[:, r]
        state = term if r == 0 else rate[r] * state + term
        local_rows.append(state)
    store_pieces(send_a, state)
    loads[2].wait()
    small[...] = jnp.zeros_like(small)
    small[0 : 2 * rows, :] = jnp.broadcast_to(
        column(lat_in[...].astype(f32)) / 256.0, (2 * rows, 128)
    )
    small[2 * rows : 2 * rows + 1, :] = wide(gain_row)

    pl.semaphore_wait(barrier, tiles - 1 + mems - 1)
    carry_copies = spread_out(1, "tile", lambda dest: send_a.at[dest], got_a)
    small_copies = spread_out(0, "tile", lambda dest: small, smalls)

    for load in loads[3:]:
        load.wait()
    east_own = wide(east_in[...].astype(f32) / 1024.0)
    north_own = wide(north_in[...].astype(f32) / 1024.0)
    edges = jnp.zeros((rows_fine, 128), f32)
    for i, wind in enumerate((east_own, north_own)):
        edges = edges + placed_at(wind, 0, 2 * halo * i, halo)
        edges = edges + placed_at(wind, band - halo, 2 * halo * i + halo, halo)
    base = 4 * halo
    for level in range(group_levels):
        slab = wide(obs_in[level])
        at = base + 2 * STEPS * level
        edges = edges + placed_at(slab, 0, at, STEPS)
        edges = edges + placed_at(slab, band - STEPS, at + STEPS, STEPS)
    halo_out[...] = edges
    halo_copies = []
    for side, d in enumerate((1, tiles - 1)):
        copy = pltpu.make_async_remote_copy(
            src_ref=halo_out,
            dst_ref=halo_in.at[side],
            send_sem=halo_send.at[side],
            recv_sem=halo_recv.at[side],
            device_id={"tile": lax.rem(t + d, tiles)},
            device_id_type=MESH,
        )
        copy.start()
        halo_copies.append(copy)
    started.extend(halo_copies)

    sub = lax.broadcasted_iota(jnp.int32, (cols, cols), 0)
    lane = lax.broadcasted_iota(jnp.int32, (cols, cols), 1)
    apart = (lane - sub).astype(f32)
    powers = jnp.exp(jnp.maximum(apart, 0.0) * math.log(LON_RATE))
    table = split(jnp.where(lane >= sub, math.sqrt(1.0 - LON_RATE**2) * powers, 0.0))

    def smooth(x, turned):
        flat = x.reshape(members * levels, cols)
        return product(split(flat), table, turned).reshape(members, levels, cols)

    smooth_rows = [smooth(x, False) for x in local_rows]

    arrive(small_copies)
    group = lax.rem(t, levels // 8)
    lane = lax.broadcasted_iota(jnp.int32, (8, 128), 1)
    sub = lax.broadcasted_iota(jnp.int32, (8, 128), 0)
    gain_mask = lane == sub + 8 * group
    gains = []
    for s in range(tiles):
        row = smalls[s, 2 * rows : 2 * rows + 1, :]
        gains.append(jnp.sum(jnp.where(gain_mask, row, 0.0), axis=1, keepdims=True))
    arrive(carry_copies)
    state = jnp.zeros((members, 8, 128), f32)
    for s in range(tiles):
        send_b[s] = state
        state = gains[s] * state + got_a[s]
    back_copies = spread_out(2, "tile", lambda dest: send_b.at[dest], got_b)

    count = lon_in.shape[1]
    lon_row = jnp.broadcast_to(lon_in[...].astype(f32) / 256.0, (8, count))
    slot = lax.broadcasted_iota(jnp.int32, (cols, 128), 0)
    lane = lax.broadcasted_iota(jnp.int32, (cols, 128), 1)
    for i in range(tiles):
        west = pltpu.roll(lon_row, (halo - band * i) % count, 1)[0:1, :128]
        lower = lax.rem(lane + (band * i - halo + count), count) // 2
        upper = lax.rem(lower + 1, cols)
        weight = jnp.where(slot == lower, west, 0.0) + jnp.where(slot == upper, 1.0 - west, 0.0)
        weight = jnp.where(lane < width, weight, 0.0)
        interp[:, 128 * i : 128 * (i + 1)] = weight.astype(jnp.bfloat16)
    arrive(halo_copies)
    from_west, from_east = halo_in[0], halo_in[1]
    for i, wind in enumerate((east_own, north_own)):
        wind_rows[i] = (
            placed_at(wind, 0, halo, band)
            + placed_at(from_west, (2 * i + 1) * halo, 0, halo)
            + placed_at(from_east, 2 * i * halo, halo + band, halo)
        )
    slabs = []
    for level in range(group_levels):
        at = base + 2 * STEPS * level
        slab = placed_at(wide(obs_in[level]), 0, halo, band)
        slab = slab + placed_at(from_west, at + STEPS, halo - STEPS, STEPS)
        slab = slab + placed_at(from_east, at, halo + band, STEPS)
        slabs.append(slab[None])
    weights[...] = jnp.swapaxes(jnp.concatenate(slabs, axis=0), 0, 1)

    arrive(back_copies)
    carried = smooth(load_pieces(got_b), False)
    gain = None
    for r in range(rows):
        gain = rate[r] if r == 0 else gain * rate[r]
        localized = gain * carried + smooth_rows[r]
        partial = spread * jnp.sum(prt[:, r].astype(f32) * localized, axis=0)
        for i in range(mems):
            parts[i, 8 * r : 8 * r + 8] = partial[i * group_levels : (i + 1) * group_levels]
    part_copies = spread_out(0, "mem", lambda dest: parts.at[dest], parts_got)
    east = expand(wind_rows.at[0], rows_fine)
    north = expand(wind_rows.at[1], rows_fine)
    east_pos = jnp.maximum(east, 0.0)
    east_neg = jnp.maximum(-east, 0.0)
    north_pos = jnp.maximum(north, 0.0)
    north_neg = jnp.maximum(-north, 0.0)
    keep = 1.0 - east_pos - east_neg - north_pos - north_neg
    lat = jnp.concatenate([expand(smalls.at[s], 2 * rows) for s in range(tiles)], axis=0)
    arrive(part_copies)
    total = parts_got[0]
    for i in range(1, mems):
        total = total + parts_got[i]
    every = product(split(total), (interp[...],), False)
    for i in range(tiles):
        rows_out[i] = every[:, 128 * i : 128 * (i + 1)]
    row_copies = spread_out(3, "tile", lambda dest: rows_out.at[dest], rows_in)
    arrive(row_copies)

    coarse = tiles * rows
    edge = jnp.zeros((1, 8, 128), f32)

    def southward(x):
        return jnp.concatenate([edge, x[:-1]], axis=0)

    def northward(x):
        return jnp.concatenate([x[1:], edge], axis=0)

    def doubled(x):
        return jnp.broadcast_to(x[:, None], (coarse, 2, 8, 128)).reshape(rows_fine, 8, 128)

    def paired(x):
        pairs = x.reshape(coarse, 2, 8, 128)
        return pairs[:, 0] + pairs[:, 1]

    def turn(x, distance):
        flat = x.reshape(rows_fine * 8, 128)
        return pltpu.roll(flat, distance, 1).reshape(rows_fine, 8, 128)

    increment = rows_in[...].reshape(coarse, 8, 128)
    g = lat * doubled(increment) + (1.0 - lat) * doubled(northward(increment))
    for _ in range(STEPS):
        g = (
            keep * g
            + east_pos * turn(g, 1)
            + east_neg * turn(g, 127)
            + north_pos * southward(g)
            + north_neg * northward(g)
        )
    g = weights[...] * g
    for _ in range(STEPS):
        g = (
            keep * g
            + turn(east_pos * g, 127)
            + turn(east_neg * g, 1)
            + northward(north_pos * g)
            + southward(north_neg * g)
        )
    lane = lax.broadcasted_iota(jnp.int32, g.shape, 2)
    g = jnp.where((lane >= halo) & (lane < halo + band), g, 0.0)
    adjoint = paired(lat * g) + southward(paired((1.0 - lat) * g))
    adj_out[...] = adjoint.reshape(tiles, rows * 8, 128)
    adj_copies = spread_out(4, "tile", lambda dest: adj_out.at[dest], adj_in)
    arrive(adj_copies)
    every = jnp.concatenate([adj_in[i] for i in range(tiles)], axis=1)
    own_adj[...] = product(split(every), (interp[...],), True)
    own_copies = spread_out(1, "mem", lambda dest: own_adj, adj_all)
    arrive(own_copies)

    member_rows = []
    for r in range(rows):
        field = jnp.concatenate([adj_all[i, 8 * r : 8 * r + 8] for i in range(mems)], axis=0)
        member_rows.append((spread * field) * prt[:, r].astype(f32))
    state = member_rows[rows - 1]
    summed = [state]
    for r in reversed(range(rows - 1)):
        state = member_rows[r] + rate[r + 1] * state
        summed.insert(0, state)
    store_pieces(send_c, rate[0] * state)
    up_copies = spread_out(5, "tile", lambda dest: send_c.at[dest], got_c)
    smooth_rows = [smooth(shrink[r] * summed[r], True) for r in range(rows)]
    arrive(up_copies)
    state = jnp.zeros((members, 8, 128), f32)
    for s in reversed(range(tiles)):
        send_d[s] = state
        state = gains[s] * state + got_c[s]
    last_copies = spread_out(6, "tile", lambda dest: send_d.at[dest], got_d)
    arrive(last_copies)
    carried = smooth(load_pieces(got_d), True)
    gain = None
    for r in reversed(range(rows)):
        gain = jnp.ones_like(rate[r]) if r == rows - 1 else gain * rate[r + 1]
        out[:, r] = ctl[:, r] + smooth_rows[r] + (shrink[r] * gain) * carried
    for copy in started:
        copy.wait_send()


def fused(
    perturbations, control, filter_rate, lat_weight, lon_weight, wind_east, wind_north, obs_weight
):
    members, levels, rows, cols = control.shape
    tiles, mems = lax.axis_size("tile"), lax.axis_size("mem")
    f32, i32 = jnp.float32, jnp.int32
    rows_fine, band = wind_east.shape
    ctl = jnp.transpose(control, (0, 2, 1, 3))
    prt = jnp.transpose(perturbations, (0, 2, 1, 3))
    group = levels // mems
    spread = float(1.0 / np.sqrt(np.float32(members * mems - 1)))
    piece = pltpu.VMEM((tiles, members, 8, 128), f32)
    partial = pltpu.VMEM((mems, rows * group, cols), f32)
    window = pltpu.VMEM((tiles, rows * group, 128), f32)
    result = pl.pallas_call(
        functools.partial(hessian_kernel, tiles, mems, spread),
        out_shape=jax.ShapeDtypeStruct(ctl.shape, f32),
        in_specs=[pl.BlockSpec(memory_space=pl.ANY)] * 8,
        out_specs=pl.BlockSpec(memory_space=pltpu.VMEM),
        scratch_shapes=[
            pltpu.VMEM(ctl.shape, f32),
            pltpu.VMEM(prt.shape, prt.dtype),
            pltpu.VMEM(filter_rate.shape, f32),
            pltpu.VMEM((1, lat_weight.shape[0]), i32),
            pltpu.VMEM((1, lon_weight.shape[0]), i32),
            pltpu.VMEM((rows_fine, band), i32),
            pltpu.VMEM((rows_fine, band), i32),
            pltpu.VMEM((group, rows_fine, band), f32),
            pltpu.VMEM((8, 128), f32),
            pltpu.VMEM((tiles, 8, 128), f32),
            pltpu.VMEM((rows_fine, 128), f32),
            pltpu.VMEM((2, rows_fine, 128), f32),
            pltpu.VMEM((2, rows_fine, 128), f32),
            pltpu.VMEM((rows_fine, group, 128), f32),
            *[piece] * 4,
            *[partial] * 2,
            *[window] * 4,
            pltpu.VMEM((rows * group, cols), f32),
            partial,
            *[piece] * 4,
            pltpu.VMEM((cols, tiles * 128), jnp.bfloat16),
            pltpu.SemaphoreType.DMA((8,)),
            pltpu.SemaphoreType.DMA((2,)),
            pltpu.SemaphoreType.DMA((2,)),
            pltpu.SemaphoreType.DMA((7, tiles)),
            pltpu.SemaphoreType.DMA((7, tiles)),
            pltpu.SemaphoreType.DMA((2, mems)),
            pltpu.SemaphoreType.DMA((2, mems)),
        ],
        compiler_params=pltpu.CompilerParams(
            collective_id=0, has_side_effects=True, vmem_limit_bytes=40 * 2**20
        ),
    )(
        ctl, prt, filter_rate, lat_weight[None], lon_weight[None], wind_east, wind_north,
        obs_weight,
    )
    return jnp.transpose(result, (0, 2, 1, 3))


def plan(
    perturbations, control, filter_rate, lat_weight, lon_weight, wind_east, wind_north, obs_weight
):
    levels, rows, cols = control.shape[1:]
    tiles, mems = lax.axis_size("tile"), lax.axis_size("mem")
    rows_fine, band = wind_east.shape
    fits = (
        levels == 8 * mems
        and levels // 8 * -(-cols // 128) == tiles
        and tiles > 2
        and 2 * rows + 1 <= 8
        and rows_fine == 2 * rows * tiles
        and rows_fine % 8 == 0
        and 2 * STEPS <= band <= 128 - 4 * STEPS
        and levels <= 128
    )
    return (fused if fits else local)(
        perturbations, control, filter_rate, lat_weight, lon_weight, wind_east, wind_north,
        obs_weight,
    )


def solution(mesh):
    placed = (
        P("mem", None, "tile", None),
        P("mem", None, "tile", None),
        P("tile", None),
        P("tile"),
        P(),
        P(None, "tile"),
        P(None, "tile"),
        P(None, None, "tile"),
    )
    return jax.shard_map(
        plan, mesh=mesh, in_specs=placed, out_specs=P("mem", None, "tile", None), check_vma=False
    )
```

```python
import functools
import math

import jax
import jax.numpy as jnp
import numpy as np
from jax import lax
from jax.experimental import pallas as pl
from jax.experimental.pallas import tpu as pltpu
from jax.sharding import PartitionSpec as P

STEPS = 3
CHUNK = 2
MESH = pl.DeviceIdType.MESH


LON_RATE = 0.8
HIGH = lax.Precision.HIGHEST


def with_halo(shard, sides, width):
    for axis, dim in sides:
        size, length = (lax.axis_size(axis), shard.shape[dim])
        up = [(i, (i + 1) % size) for i in range(size)]
        down = [(j, i) for i, j in up]
        last = lax.slice_in_dim(shard, length - width, length, axis=dim)
        leading = lax.slice_in_dim(shard, 0, width, axis=dim)
        before = lax.ppermute(last, axis, up)
        after = lax.ppermute(leading, axis, down)
        shard = jnp.concatenate([before, shard, after], axis=dim)
    return shard


def carried_in(part, axis, combine, identity, reverse):
    count = lax.axis_size(axis)
    place = lax.axis_index(axis)
    ahead = count - 1 - place if reverse else place
    gathered = jax.tree.map(lambda a: lax.all_gather(a, axis), part)
    state = jax.tree.map(lambda a, e: jnp.zeros_like(a) + jnp.asarray(e, a.dtype), part, identity)

    def one(turn, state):
        source = count - 1 - turn if reverse else turn
        return combine(
            state, jax.tree.map(lambda a: lax.dynamic_index_in_dim(a, source, 0, False), gathered)
        )

    return lax.fori_loop(0, ahead, one, state)


def shifted(block, axis, distance):
    devices = range(lax.axis_size(axis))
    route = [(i - distance, i) for i in devices if i - distance in devices]
    return lax.ppermute(block, axis, route)


def lon_table(col_count):
    across = jnp.arange(col_count)
    distance = across[None, :] - across[:, None]
    weight_scale = jnp.sqrt(jnp.float32(1.0 - LON_RATE * LON_RATE))
    powers = jnp.power(jnp.float32(LON_RATE), jnp.maximum(distance, 0).astype(jnp.float32))
    return jnp.where(distance >= 0, weight_scale * powers, jnp.float32(0.0))


def wind_terms(wind_east, wind_north):
    east_rate = wind_east.astype(jnp.float32) / 1024.0
    north_rate = wind_north.astype(jnp.float32) / 1024.0
    east_pos = jnp.maximum(east_rate, 0.0)
    east_neg = jnp.maximum(-east_rate, 0.0)
    north_pos = jnp.maximum(north_rate, 0.0)
    north_neg = jnp.maximum(-north_rate, 0.0)
    keep = 1.0 - east_pos - east_neg - north_pos - north_neg
    return (east_pos, east_neg, north_pos, north_neg, keep)


def compose(earlier, later):
    return (earlier[0] * later[0], later[0][None, :, None] * earlier[1] + later[1])


def advance(field_now, coeffs):
    east_pos, east_neg, north_pos, north_neg, keep = coeffs
    padded = with_halo(field_now, (("tile", 1),), 1)
    rows_pad = jnp.pad(field_now, ((0, 0), (0, 0), (1, 1)))
    result = keep * field_now + east_pos * padded[:, :-2, :] + east_neg * padded[:, 2:, :]
    return result + north_pos * rows_pad[:, :, :-2] + north_neg * rows_pad[:, :, 2:]


def retreat(field_now, coeffs):
    east_pos, east_neg, north_pos, north_neg, keep = coeffs
    padded = with_halo(field_now, (("tile", 1),), 1)
    from_east = east_pos[2:, :] * padded[:, 2:, :]
    from_west = east_neg[:-2, :] * padded[:, :-2, :]
    from_south = jnp.pad(north_pos[1:-1, :] * field_now, ((0, 0), (0, 0), (0, 1)))[:, :, 1:]
    from_north = jnp.pad(north_neg[1:-1, :] * field_now, ((0, 0), (0, 0), (1, 0)))[:, :, :-1]
    return keep[1:-1, :] * field_now + from_east + from_west + from_south + from_north


def local(
    perturbations, control, filter_rate, lat_weight, lon_weight, wind_east, wind_north, obs_weight
):
    member_count, level_count, coarse_rows, col_count = control.shape
    filter_table = lon_table(col_count)
    shrink = jnp.sqrt(1.0 - filter_rate * filter_rate)
    spread = 1.0 / jnp.sqrt(jnp.float32(member_count * lax.axis_size("mem") - 1))
    start_pair = (
        jnp.ones((level_count,), jnp.float32),
        jnp.zeros((member_count, level_count, col_count), jnp.float32),
    )
    smoothed = jnp.einsum("mvrc,cd->rmvd", control, filter_table, precision=HIGH)

    def forward_row(pair_now, inputs):
        gain_now, stretch = pair_now
        rate_row, shrink_row, row_vals = inputs
        gain_now = rate_row * gain_now
        stretch = rate_row[None, :, None] * stretch + shrink_row[None, :, None] * row_vals
        return ((gain_now, stretch), (gain_now, stretch))

    summary, (gains, stretches) = lax.scan(forward_row, start_pair, (filter_rate, shrink, smoothed))
    _, incoming = carried_in(summary, "tile", compose, start_pair, False)
    localized = gains[:, None, :, None] * incoming[None] + stretches
    partial_sum = spread * jnp.einsum(
        "mvrc,rmvc->vrc", perturbations.astype(jnp.float32), localized, precision=HIGH
    )
    increment = lax.psum(partial_sum, "mem")
    weight_here = obs_weight
    weight_here = jnp.swapaxes(weight_here, 1, 2)
    winds_turned = jnp.stack([jnp.transpose(wind_east), jnp.transpose(wind_north)])
    wind_halo = with_halo(winds_turned, (("tile", 1),), 1)
    halo_coeffs = wind_terms(wind_halo[0], wind_halo[1])
    inner_coeffs = tuple((term_item[1:-1, :] for term_item in halo_coeffs))
    level_here = increment.shape[0]
    tile_count = lax.axis_size("tile")
    band_cols = wind_east.shape[1]
    next_first = shifted(increment[:, :1, :], "tile", -1)
    window = band_cols // 2 + 2
    starts = jnp.arange(tile_count) * band_cols // 2
    cols_index = (starts[:, None] + jnp.arange(window)[None, :]) % col_count
    select = (jnp.arange(col_count)[:, None, None] == cols_index[None]).astype(jnp.float32)
    extended = jnp.concatenate([increment, next_first], axis=1)
    windows = jnp.einsum("vrc,cnk->vnrk", extended, select, precision=HIGH)
    arrived = lax.all_to_all(windows, "tile", split_axis=1, concat_axis=1, tiled=True)
    lat_every = lax.all_gather(lat_weight, "tile", axis=0, tiled=True)
    frac_every = (lat_every.astype(jnp.float32) / 256.0).reshape(1, tile_count, 2 * coarse_rows, 1)
    lower_rows = jnp.repeat(arrived[:, :, :-1, :], 2, axis=2)
    higher_rows = jnp.repeat(arrived[:, :, 1:, :], 2, axis=2)
    fine_window = (frac_every * lower_rows + (1.0 - frac_every) * higher_rows).reshape(
        level_here, tile_count * 2 * coarse_rows, window
    )
    first_col = lax.axis_index("tile") * band_cols
    fractions = (
        lax.dynamic_slice_in_dim(lon_weight, first_col, band_cols, 0).astype(jnp.float32) / 256.0
    )
    lower_local = (first_col + jnp.arange(band_cols)) // 2 - first_col // 2
    slots = jnp.arange(window)[:, None]
    band_interp = jnp.where(
        slots == lower_local[None, :], fractions[None, :], jnp.float32(0.0)
    ) + jnp.where(slots == lower_local[None, :] + 1, 1.0 - fractions[None, :], jnp.float32(0.0))
    field_now = jnp.einsum("vqk,kj->vjq", fine_window, band_interp, precision=HIGH)
    for step_index in range(STEPS):
        field_now = advance(field_now, inner_coeffs)
    field_now = weight_here * field_now
    for step_index in range(STEPS):
        field_now = retreat(field_now, halo_coeffs)
    rows_window = jnp.einsum("vjq,kj->vqk", field_now, band_interp, precision=HIGH).reshape(
        level_here, tile_count, 2 * coarse_rows, window
    )
    own_window = (
        (frac_every * rows_window)
        .reshape(level_here, tile_count, coarse_rows, 2, window)
        .sum(axis=3)
    )
    above_window = (
        ((1.0 - frac_every) * rows_window)
        .reshape(level_here, tile_count, coarse_rows, 2, window)
        .sum(axis=3)
    )
    extended_adjoint = jnp.pad(own_window, ((0, 0), (0, 0), (0, 1), (0, 0))) + jnp.pad(
        above_window, ((0, 0), (0, 0), (1, 0), (0, 0))
    )
    returned = lax.all_to_all(extended_adjoint, "tile", split_axis=1, concat_axis=1, tiled=True)
    column_sums = jnp.einsum("vnrk,cnk->vrc", returned, select, precision=HIGH)
    base_part = column_sums[:, :coarse_rows, :]
    edge_row = column_sums[:, coarse_rows:, :]
    carried = shifted(edge_row, "tile", 1)
    increment_adjoint = base_part + jnp.concatenate(
        [carried, jnp.zeros((level_here, coarse_rows - 1, col_count), jnp.float32)], axis=1
    )
    member_adjoint = spread * jnp.einsum(
        "mvrc,vrc->rmvc", perturbations.astype(jnp.float32), increment_adjoint, precision=HIGH
    )

    def backward_row(pair_now, inputs):
        gain_now, stretch = pair_now
        rate_row, row_vals = inputs
        outputs_here = (gain_now, stretch)
        gain_now = rate_row * gain_now
        stretch = rate_row[None, :, None] * (row_vals + stretch)
        return ((gain_now, stretch), outputs_here)

    summary_up, (gains_up, stretches_up) = lax.scan(
        backward_row, start_pair, (filter_rate, member_adjoint), reverse=True
    )
    _, incoming_up = carried_in(summary_up, "tile", compose, start_pair, True)
    summed = member_adjoint + gains_up[:, None, :, None] * incoming_up[None] + stretches_up
    scaled = summed * shrink[:, None, :, None]
    return control + jnp.einsum("rmvd,cd->mvrc", scaled, filter_table, precision=HIGH)

def split(x):
    high = x.astype(jnp.bfloat16)
    return high, (x - high.astype(jnp.float32)).astype(jnp.bfloat16)


def product(a, b, turned):
    dims = (((1,), (1 if turned else 0,)), ((), ()))

    def one(left, right):
        return lax.dot_general(left, right, dims, preferred_element_type=jnp.float32)

    total = None
    for i, left in enumerate(a):
        for j, right in enumerate(b):
            if i + j < 2:
                term = one(left, right)
                total = term if total is None else total + term
    return total


def expand(ref, count):
    return jnp.concatenate(
        [jnp.broadcast_to(ref[q : q + 1, :], (8, 128))[None] for q in range(count)], axis=0
    )


def wide(x):
    pad = jnp.zeros(x.shape[:-1] + (128 - x.shape[-1],), x.dtype)
    return jnp.concatenate([x, pad], axis=x.ndim - 1)


def placed_at(x, source, target, width):
    moved = pltpu.roll(x, (target - source) % 128, 1)
    lane = lax.broadcasted_iota(jnp.int32, x.shape, 1)
    return jnp.where((lane >= target) & (lane < target + width), moved, 0.0)


def column(row):
    count = row.shape[1]
    sub = lax.broadcasted_iota(jnp.int32, (count, count), 0)
    lane = lax.broadcasted_iota(jnp.int32, (count, count), 1)
    return jnp.sum(jnp.where(sub == lane, row, 0.0), axis=1, keepdims=True)


def hessian_kernel(
    tiles, mems, spread,
    ctl_hbm, prt_hbm, rates_hbm, lat_hbm, lon_hbm, east_hbm, north_hbm, obs_hbm,
    out,
    ctl, prt, rates, lat_in, lon_in, east_in, north_in, obs_in,
    small, smalls, halo_out, halo_in, wind_rows, weights, send_a, got_a, send_b, got_b,
    parts, parts_got, rows_out, rows_in, adj_out, adj_in, own_adj, adj_all,
    send_c, got_c, send_d, got_d, interp,
    local_sem, halo_send, halo_recv, tile_send, tile_recv, mem_send, mem_recv,
):
    members, rows, levels, cols = ctl.shape
    t = lax.axis_index("tile")
    m = lax.axis_index("mem")
    f32 = jnp.float32
    started = []
    group_levels = levels // mems
    rows_fine, band = east_in.shape
    halo = 2 * STEPS
    width = band + 2 * halo
    chunks = [(i, min(i + CHUNK, members)) for i in range(0, members, CHUNK)]

    loads = []
    sources = (
        (rates_hbm, rates), (ctl_hbm, ctl), (lat_hbm, lat_in), (east_hbm, east_in),
        (north_hbm, north_in), (obs_hbm.at[pl.ds(m * group_levels, group_levels)], obs_in),
        (lon_hbm, lon_in), (prt_hbm, prt),
    )
    for i, (source, target) in enumerate(sources):
        load = pltpu.make_async_copy(source, target, local_sem.at[i])
        load.start()
        loads.append(load)

    barrier = pltpu.get_barrier_semaphore()
    for d in range(1, tiles):
        pl.semaphore_signal(
            barrier, inc=1, device_id={"tile": lax.rem(t + d, tiles)}, device_id_type=MESH
        )
    for d in range(1, mems):
        pl.semaphore_signal(
            barrier, inc=1, device_id={"mem": lax.rem(m + d, mems)}, device_id_type=MESH
        )

    def spread_out(kind, axis, source, target, place=lambda ref, me: ref.at[me]):
        size, me = (tiles, t) if axis == "tile" else (mems, m)
        sends, recvs = (tile_send, tile_recv) if axis == "tile" else (mem_send, mem_recv)
        copies = []
        for d in range(1, size):
            dest = lax.rem(me + d, size)
            copy = pltpu.make_async_remote_copy(
                src_ref=source(dest),
                dst_ref=place(target, me),
                send_sem=sends.at[kind, d],
                recv_sem=recvs.at[kind, d],
                device_id={axis: dest},
                device_id_type=MESH,
            )
            copy.start()
            copies.append(copy)
        place(target, me)[...] = source(me)[...]
        started.extend(copies)
        return copies

    def exchange(kind, chunk, source, target):
        low, high = chunks[chunk]
        span = pl.ds(low, high - low)
        return spread_out(
            3 + kind * len(chunks) + chunk,
            "tile",
            lambda dest: source.at[dest, span],
            target,
            lambda ref, me: ref.at[me, span],
        )

    def arrive(copies):
        for copy in copies:
            copy.wait_recv()

    def store_pieces(target, value, low, high):
        for lane_part in range(-(-cols // 128)):
            at = 128 * lane_part
            span = min(128, cols - at)
            for group in range(levels // 8):
                piece = lane_part * (levels // 8) + group
                block = value[:, 8 * group : 8 * group + 8, at : at + span]
                target[piece, low:high] = wide(block) if span < 128 else block

    def load_pieces(source, low, high):
        groups = levels // 8
        lanes = []
        for lane_part in range(-(-cols // 128)):
            span = min(128, cols - 128 * lane_part)
            blocks = [source[lane_part * groups + g, low:high] for g in range(groups)]
            lanes.append(jnp.concatenate(blocks, axis=1)[:, :, :span])
        return jnp.concatenate(lanes, axis=2)

    loads[0].wait()
    rate = [column(rates[r : r + 1, :]) for r in range(rows)]
    shrink = [jnp.sqrt(1.0 - a * a) for a in rate]
    gain_row = rates[0:1, :]
    for r in range(1, rows):
        gain_row = gain_row * rates[r : r + 1, :]
    loads[2].wait()
    small[...] = jnp.zeros_like(small)
    small[0 : 2 * rows, :] = jnp.broadcast_to(
        column(lat_in[...].astype(f32)) / 256.0, (2 * rows, 128)
    )
    small[2 * rows : 2 * rows + 1, :] = wide(gain_row)

    pl.semaphore_wait(barrier, tiles - 1 + mems - 1)
    small_copies = spread_out(0, "tile", lambda dest: small, smalls)
    loads[1].wait()
    local_rows = []
    carry_copies = []
    for c, (low, high) in enumerate(chunks):
        state = None
        states = []
        for r in range(rows):
            term = shrink[r] * ctl[low:high, r]
            state = term if r == 0 else rate[r] * state + term
            states.append(state)
        local_rows.append(states)
        store_pieces(send_a, state, low, high)
        carry_copies.append(exchange(0, c, send_a, got_a))

    for load in loads[3:]:
        load.wait()
    east_own = wide(east_in[...].astype(f32) / 1024.0)
    north_own = wide(north_in[...].astype(f32) / 1024.0)
    edges = jnp.zeros((rows_fine, 128), f32)
    for i, wind in enumerate((east_own, north_own)):
        edges = edges + placed_at(wind, 0, 2 * halo * i, halo)
        edges = edges + placed_at(wind, band - halo, 2 * halo * i + halo, halo)
    base = 4 * halo
    for level in range(group_levels):
        slab = wide(obs_in[level])
        at = base + 2 * STEPS * level
        edges = edges + placed_at(slab, 0, at, STEPS)
        edges = edges + placed_at(slab, band - STEPS, at + STEPS, STEPS)
    halo_out[...] = edges
    halo_copies = []
    for side, d in enumerate((1, tiles - 1)):
        copy = pltpu.make_async_remote_copy(
            src_ref=halo_out,
            dst_ref=halo_in.at[side],
            send_sem=halo_send.at[side],
            recv_sem=halo_recv.at[side],
            device_id={"tile": lax.rem(t + d, tiles)},
            device_id_type=MESH,
        )
        copy.start()
        halo_copies.append(copy)
    started.extend(halo_copies)

    sub = lax.broadcasted_iota(jnp.int32, (cols, cols), 0)
    lane = lax.broadcasted_iota(jnp.int32, (cols, cols), 1)
    apart = (lane - sub).astype(f32)
    powers = jnp.exp(jnp.maximum(apart, 0.0) * math.log(LON_RATE))
    table = split(jnp.where(lane >= sub, math.sqrt(1.0 - LON_RATE**2) * powers, 0.0))

    def smooth(x, turned):
        flat = x.reshape(x.shape[0] * levels, cols)
        return product(split(flat), table, turned).reshape(x.shape)

    smooth_rows = [[smooth(x, False) for x in states] for states in local_rows]

    arrive(small_copies)
    group = lax.rem(t, levels // 8)
    lane = lax.broadcasted_iota(jnp.int32, (8, 128), 1)
    sub = lax.broadcasted_iota(jnp.int32, (8, 128), 0)
    gain_mask = lane == sub + 8 * group
    gains = []
    for s in range(tiles):
        row = smalls[s, 2 * rows : 2 * rows + 1, :]
        gains.append(jnp.sum(jnp.where(gain_mask, row, 0.0), axis=1, keepdims=True))
    back_copies = []
    for c, (low, high) in enumerate(chunks):
        arrive(carry_copies[c])
        state = jnp.zeros((high - low, 8, 128), f32)
        for s in range(tiles):
            send_b[s, low:high] = state
            state = gains[s] * state + got_a[s, low:high]
        back_copies.append(exchange(1, c, send_b, got_b))

    count = lon_in.shape[0]
    lon_row = jnp.broadcast_to(lon_in[...].astype(f32)[None] / 256.0, (8, count))
    slot = lax.broadcasted_iota(jnp.int32, (cols, 128), 0)
    lane = lax.broadcasted_iota(jnp.int32, (cols, 128), 1)
    for i in range(tiles):
        west = pltpu.roll(lon_row, (halo - band * i) % count, 1)[0:1, :128]
        lower = lax.rem(lane + (band * i - halo + count), count) // 2
        upper = lax.rem(lower + 1, cols)
        weight = jnp.where(slot == lower, west, 0.0) + jnp.where(slot == upper, 1.0 - west, 0.0)
        weight = jnp.where(lane < width, weight, 0.0)
        interp[:, 128 * i : 128 * (i + 1)] = weight.astype(jnp.bfloat16)
    arrive(halo_copies)
    from_west, from_east = halo_in[0], halo_in[1]
    for i, wind in enumerate((east_own, north_own)):
        wind_rows[i] = (
            placed_at(wind, 0, halo, band)
            + placed_at(from_west, (2 * i + 1) * halo, 0, halo)
            + placed_at(from_east, 2 * i * halo, halo + band, halo)
        )
    slabs = []
    for level in range(group_levels):
        at = base + 2 * STEPS * level
        slab = placed_at(wide(obs_in[level]), 0, halo, band)
        slab = slab + placed_at(from_west, at + STEPS, halo - STEPS, STEPS)
        slab = slab + placed_at(from_east, at, halo + band, STEPS)
        slabs.append(slab[None])
    weights[...] = jnp.swapaxes(jnp.concatenate(slabs, axis=0), 0, 1)

    partial = [jnp.zeros((levels, cols), f32)] * rows
    for c, (low, high) in enumerate(chunks):
        arrive(back_copies[c])
        carried = smooth(load_pieces(got_b, low, high), False)
        gain = None
        for r in range(rows):
            gain = rate[r] if r == 0 else gain * rate[r]
            localized = gain * carried + smooth_rows[c][r]
            partial[r] = partial[r] + jnp.sum(prt[low:high, r].astype(f32) * localized, axis=0)
    for r in range(rows):
        for i in range(mems):
            parts[i, 8 * r : 8 * r + 8] = (
                spread * partial[r][i * group_levels : (i + 1) * group_levels]
            )
    part_copies = spread_out(0, "mem", lambda dest: parts.at[dest], parts_got)
    east = expand(wind_rows.at[0], rows_fine)
    north = expand(wind_rows.at[1], rows_fine)
    east_pos = jnp.maximum(east, 0.0)
    east_neg = jnp.maximum(-east, 0.0)
    north_pos = jnp.maximum(north, 0.0)
    north_neg = jnp.maximum(-north, 0.0)
    keep = 1.0 - east_pos - east_neg - north_pos - north_neg
    lat = jnp.concatenate([expand(smalls.at[s], 2 * rows) for s in range(tiles)], axis=0)
    arrive(part_copies)
    total = parts_got[0]
    for i in range(1, mems):
        total = total + parts_got[i]
    every = product(split(total), (interp[...],), False)
    for i in range(tiles):
        rows_out[i] = every[:, 128 * i : 128 * (i + 1)]
    row_copies = spread_out(1, "tile", lambda dest: rows_out.at[dest], rows_in)
    arrive(row_copies)

    coarse = tiles * rows
    edge = jnp.zeros((1, 8, 128), f32)

    def southward(x):
        return jnp.concatenate([edge, x[:-1]], axis=0)

    def northward(x):
        return jnp.concatenate([x[1:], edge], axis=0)

    def doubled(x):
        return jnp.broadcast_to(x[:, None], (coarse, 2, 8, 128)).reshape(rows_fine, 8, 128)

    def paired(x):
        pairs = x.reshape(coarse, 2, 8, 128)
        return pairs[:, 0] + pairs[:, 1]

    def turn(x, distance):
        flat = x.reshape(rows_fine * 8, 128)
        return pltpu.roll(flat, distance, 1).reshape(rows_fine, 8, 128)

    increment = rows_in[...].reshape(coarse, 8, 128)
    g = lat * doubled(increment) + (1.0 - lat) * doubled(northward(increment))
    for _ in range(STEPS):
        g = (
            keep * g
            + east_pos * turn(g, 1)
            + east_neg * turn(g, 127)
            + north_pos * southward(g)
            + north_neg * northward(g)
        )
    g = weights[...] * g
    for _ in range(STEPS):
        g = (
            keep * g
            + turn(east_pos * g, 127)
            + turn(east_neg * g, 1)
            + northward(north_pos * g)
            + southward(north_neg * g)
        )
    lane = lax.broadcasted_iota(jnp.int32, g.shape, 2)
    g = jnp.where((lane >= halo) & (lane < halo + band), g, 0.0)
    adjoint = paired(lat * g) + southward(paired((1.0 - lat) * g))
    adj_out[...] = adjoint.reshape(tiles, rows * 8, 128)
    adj_copies = spread_out(2, "tile", lambda dest: adj_out.at[dest], adj_in)
    arrive(adj_copies)
    every = jnp.concatenate([adj_in[i] for i in range(tiles)], axis=1)
    own_adj[...] = product(split(every), (interp[...],), True)
    own_copies = spread_out(1, "mem", lambda dest: own_adj, adj_all)
    arrive(own_copies)

    fields = []
    for r in range(rows):
        field = jnp.concatenate([adj_all[i, 8 * r : 8 * r + 8] for i in range(mems)], axis=0)
        fields.append(spread * field)
    summed = []
    up_copies = []
    for c, (low, high) in enumerate(chunks):
        state = None
        states = []
        for r in reversed(range(rows)):
            term = fields[r] * prt[low:high, r].astype(f32)
            state = term if r == rows - 1 else term + rate[r + 1] * state
            states.insert(0, state)
        summed.append(states)
        store_pieces(send_c, rate[0] * state, low, high)
        up_copies.append(exchange(2, c, send_c, got_c))
    smooth_rows = [
        [smooth(shrink[r] * states[r], True) for r in range(rows)] for states in summed
    ]
    last_copies = []
    for c, (low, high) in enumerate(chunks):
        arrive(up_copies[c])
        state = jnp.zeros((high - low, 8, 128), f32)
        for s in reversed(range(tiles)):
            send_d[s, low:high] = state
            state = gains[s] * state + got_c[s, low:high]
        last_copies.append(exchange(3, c, send_d, got_d))
    for c, (low, high) in enumerate(chunks):
        arrive(last_copies[c])
        carried = smooth(load_pieces(got_d, low, high), True)
        gain = None
        for r in reversed(range(rows)):
            gain = jnp.ones_like(rate[r]) if r == rows - 1 else gain * rate[r + 1]
            out[low:high, r] = (
                ctl[low:high, r] + smooth_rows[c][r] + (shrink[r] * gain) * carried
            )
    for copy in started:
        copy.wait_send()


def fused(
    perturbations, control, filter_rate, lat_weight, lon_weight, wind_east, wind_north, obs_weight
):
    members, levels, rows, cols = control.shape
    tiles, mems = lax.axis_size("tile"), lax.axis_size("mem")
    f32, i32 = jnp.float32, jnp.int32
    rows_fine, band = wind_east.shape
    ctl = jnp.transpose(control, (0, 2, 1, 3))
    prt = jnp.transpose(perturbations, (0, 2, 1, 3))
    group = levels // mems
    spread = float(1.0 / np.sqrt(np.float32(members * mems - 1)))
    kinds = 3 + 4 * -(-members // CHUNK)
    piece = pltpu.VMEM((tiles, members, 8, 128), f32)
    partial = pltpu.VMEM((mems, rows * group, cols), f32)
    window = pltpu.VMEM((tiles, rows * group, 128), f32)
    result = pl.pallas_call(
        functools.partial(hessian_kernel, tiles, mems, spread),
        out_shape=jax.ShapeDtypeStruct(ctl.shape, f32),
        in_specs=[pl.BlockSpec(memory_space=pltpu.HBM)] * 8,
        out_specs=pl.BlockSpec(memory_space=pltpu.VMEM),
        scratch_shapes=[
            pltpu.VMEM(ctl.shape, f32),
            pltpu.VMEM(prt.shape, prt.dtype),
            pltpu.VMEM(filter_rate.shape, f32),
            pltpu.VMEM((1, lat_weight.shape[0]), i32),
            pltpu.VMEM(lon_weight.shape, i32),
            pltpu.VMEM((rows_fine, band), i32),
            pltpu.VMEM((rows_fine, band), i32),
            pltpu.VMEM((group, rows_fine, band), f32),
            pltpu.VMEM((8, 128), f32),
            pltpu.VMEM((tiles, 8, 128), f32),
            pltpu.VMEM((rows_fine, 128), f32),
            pltpu.VMEM((2, rows_fine, 128), f32),
            pltpu.VMEM((2, rows_fine, 128), f32),
            pltpu.VMEM((rows_fine, group, 128), f32),
            *[piece] * 4,
            *[partial] * 2,
            *[window] * 4,
            pltpu.VMEM((rows * group, cols), f32),
            partial,
            *[piece] * 4,
            pltpu.VMEM((cols, tiles * 128), jnp.bfloat16),
            pltpu.SemaphoreType.DMA((8,)),
            pltpu.SemaphoreType.DMA((2,)),
            pltpu.SemaphoreType.DMA((2,)),
            pltpu.SemaphoreType.DMA((kinds, tiles)),
            pltpu.SemaphoreType.DMA((kinds, tiles)),
            pltpu.SemaphoreType.DMA((2, mems)),
            pltpu.SemaphoreType.DMA((2, mems)),
        ],
        compiler_params=pltpu.CompilerParams(
            collective_id=0, has_side_effects=True, vmem_limit_bytes=60 * 2**20
        ),
    )(
        ctl, prt, filter_rate, lat_weight[None], lon_weight, wind_east, wind_north,
        obs_weight,
    )
    return jnp.transpose(result, (0, 2, 1, 3))


def plan(
    perturbations, control, filter_rate, lat_weight, lon_weight, wind_east, wind_north, obs_weight
):
    levels, rows, cols = control.shape[1:]
    tiles, mems = lax.axis_size("tile"), lax.axis_size("mem")
    rows_fine, band = wind_east.shape
    fits = (
        levels == 8 * mems
        and levels // 8 * -(-cols // 128) == tiles
        and tiles > 2
        and 2 * rows + 1 <= 8
        and rows_fine == 2 * rows * tiles
        and rows_fine % 8 == 0
        and 2 * STEPS <= band <= 128 - 4 * STEPS
        and levels <= 128
    )
    return (fused if fits else local)(
        perturbations, control, filter_rate, lat_weight, lon_weight, wind_east, wind_north,
        obs_weight,
    )


def solution(mesh):
    placed = (
        P("mem", None, "tile", None),
        P("mem", None, "tile", None),
        P("tile", None),
        P("tile"),
        P(),
        P(None, "tile"),
        P(None, "tile"),
        P(None, None, "tile"),
    )
    return jax.shard_map(
        plan, mesh=mesh, in_specs=placed, out_specs=P("mem", None, "tile", None), check_vma=False
    )
```

```python
import functools
import math

import jax
import jax.numpy as jnp
import numpy as np
from jax import lax
from jax.experimental import pallas as pl
from jax.experimental.pallas import tpu as pltpu
from jax.sharding import PartitionSpec as P

STEPS = 3
CHUNK = 2
MESH = pl.DeviceIdType.MESH


LON_RATE = 0.8
HIGH = lax.Precision.HIGHEST


def with_halo(shard, sides, width):
    for axis, dim in sides:
        size, length = (lax.axis_size(axis), shard.shape[dim])
        up = [(i, (i + 1) % size) for i in range(size)]
        down = [(j, i) for i, j in up]
        last = lax.slice_in_dim(shard, length - width, length, axis=dim)
        leading = lax.slice_in_dim(shard, 0, width, axis=dim)
        before = lax.ppermute(last, axis, up)
        after = lax.ppermute(leading, axis, down)
        shard = jnp.concatenate([before, shard, after], axis=dim)
    return shard


def carried_in(part, axis, combine, identity, reverse):
    count = lax.axis_size(axis)
    place = lax.axis_index(axis)
    ahead = count - 1 - place if reverse else place
    gathered = jax.tree.map(lambda a: lax.all_gather(a, axis), part)
    state = jax.tree.map(lambda a, e: jnp.zeros_like(a) + jnp.asarray(e, a.dtype), part, identity)

    def one(turn, state):
        source = count - 1 - turn if reverse else turn
        return combine(
            state, jax.tree.map(lambda a: lax.dynamic_index_in_dim(a, source, 0, False), gathered)
        )

    return lax.fori_loop(0, ahead, one, state)


def shifted(block, axis, distance):
    devices = range(lax.axis_size(axis))
    route = [(i - distance, i) for i in devices if i - distance in devices]
    return lax.ppermute(block, axis, route)


def lon_table(col_count):
    across = jnp.arange(col_count)
    distance = across[None, :] - across[:, None]
    weight_scale = jnp.sqrt(jnp.float32(1.0 - LON_RATE * LON_RATE))
    powers = jnp.power(jnp.float32(LON_RATE), jnp.maximum(distance, 0).astype(jnp.float32))
    return jnp.where(distance >= 0, weight_scale * powers, jnp.float32(0.0))


def wind_terms(wind_east, wind_north):
    east_rate = wind_east.astype(jnp.float32) / 1024.0
    north_rate = wind_north.astype(jnp.float32) / 1024.0
    east_pos = jnp.maximum(east_rate, 0.0)
    east_neg = jnp.maximum(-east_rate, 0.0)
    north_pos = jnp.maximum(north_rate, 0.0)
    north_neg = jnp.maximum(-north_rate, 0.0)
    keep = 1.0 - east_pos - east_neg - north_pos - north_neg
    return (east_pos, east_neg, north_pos, north_neg, keep)


def compose(earlier, later):
    return (earlier[0] * later[0], later[0][None, :, None] * earlier[1] + later[1])


def advance(field_now, coeffs):
    east_pos, east_neg, north_pos, north_neg, keep = coeffs
    padded = with_halo(field_now, (("tile", 1),), 1)
    rows_pad = jnp.pad(field_now, ((0, 0), (0, 0), (1, 1)))
    result = keep * field_now + east_pos * padded[:, :-2, :] + east_neg * padded[:, 2:, :]
    return result + north_pos * rows_pad[:, :, :-2] + north_neg * rows_pad[:, :, 2:]


def retreat(field_now, coeffs):
    east_pos, east_neg, north_pos, north_neg, keep = coeffs
    padded = with_halo(field_now, (("tile", 1),), 1)
    from_east = east_pos[2:, :] * padded[:, 2:, :]
    from_west = east_neg[:-2, :] * padded[:, :-2, :]
    from_south = jnp.pad(north_pos[1:-1, :] * field_now, ((0, 0), (0, 0), (0, 1)))[:, :, 1:]
    from_north = jnp.pad(north_neg[1:-1, :] * field_now, ((0, 0), (0, 0), (1, 0)))[:, :, :-1]
    return keep[1:-1, :] * field_now + from_east + from_west + from_south + from_north


def local(
    perturbations, control, filter_rate, lat_weight, lon_weight, wind_east, wind_north, obs_weight
):
    member_count, level_count, coarse_rows, col_count = control.shape
    filter_table = lon_table(col_count)
    shrink = jnp.sqrt(1.0 - filter_rate * filter_rate)
    spread = 1.0 / jnp.sqrt(jnp.float32(member_count * lax.axis_size("mem") - 1))
    start_pair = (
        jnp.ones((level_count,), jnp.float32),
        jnp.zeros((member_count, level_count, col_count), jnp.float32),
    )
    smoothed = jnp.einsum("mvrc,cd->rmvd", control, filter_table, precision=HIGH)

    def forward_row(pair_now, inputs):
        gain_now, stretch = pair_now
        rate_row, shrink_row, row_vals = inputs
        gain_now = rate_row * gain_now
        stretch = rate_row[None, :, None] * stretch + shrink_row[None, :, None] * row_vals
        return ((gain_now, stretch), (gain_now, stretch))

    summary, (gains, stretches) = lax.scan(forward_row, start_pair, (filter_rate, shrink, smoothed))
    _, incoming = carried_in(summary, "tile", compose, start_pair, False)
    localized = gains[:, None, :, None] * incoming[None] + stretches
    partial_sum = spread * jnp.einsum(
        "mvrc,rmvc->vrc", perturbations.astype(jnp.float32), localized, precision=HIGH
    )
    increment = lax.psum(partial_sum, "mem")
    weight_here = obs_weight
    weight_here = jnp.swapaxes(weight_here, 1, 2)
    winds_turned = jnp.stack([jnp.transpose(wind_east), jnp.transpose(wind_north)])
    wind_halo = with_halo(winds_turned, (("tile", 1),), 1)
    halo_coeffs = wind_terms(wind_halo[0], wind_halo[1])
    inner_coeffs = tuple((term_item[1:-1, :] for term_item in halo_coeffs))
    level_here = increment.shape[0]
    tile_count = lax.axis_size("tile")
    band_cols = wind_east.shape[1]
    next_first = shifted(increment[:, :1, :], "tile", -1)
    window = band_cols // 2 + 2
    starts = jnp.arange(tile_count) * band_cols // 2
    cols_index = (starts[:, None] + jnp.arange(window)[None, :]) % col_count
    select = (jnp.arange(col_count)[:, None, None] == cols_index[None]).astype(jnp.float32)
    extended = jnp.concatenate([increment, next_first], axis=1)
    windows = jnp.einsum("vrc,cnk->vnrk", extended, select, precision=HIGH)
    arrived = lax.all_to_all(windows, "tile", split_axis=1, concat_axis=1, tiled=True)
    lat_every = lax.all_gather(lat_weight, "tile", axis=0, tiled=True)
    frac_every = (lat_every.astype(jnp.float32) / 256.0).reshape(1, tile_count, 2 * coarse_rows, 1)
    lower_rows = jnp.repeat(arrived[:, :, :-1, :], 2, axis=2)
    higher_rows = jnp.repeat(arrived[:, :, 1:, :], 2, axis=2)
    fine_window = (frac_every * lower_rows + (1.0 - frac_every) * higher_rows).reshape(
        level_here, tile_count * 2 * coarse_rows, window
    )
    first_col = lax.axis_index("tile") * band_cols
    fractions = (
        lax.dynamic_slice_in_dim(lon_weight, first_col, band_cols, 0).astype(jnp.float32) / 256.0
    )
    lower_local = (first_col + jnp.arange(band_cols)) // 2 - first_col // 2
    slots = jnp.arange(window)[:, None]
    band_interp = jnp.where(
        slots == lower_local[None, :], fractions[None, :], jnp.float32(0.0)
    ) + jnp.where(slots == lower_local[None, :] + 1, 1.0 - fractions[None, :], jnp.float32(0.0))
    field_now = jnp.einsum("vqk,kj->vjq", fine_window, band_interp, precision=HIGH)
    for step_index in range(STEPS):
        field_now = advance(field_now, inner_coeffs)
    field_now = weight_here * field_now
    for step_index in range(STEPS):
        field_now = retreat(field_now, halo_coeffs)
    rows_window = jnp.einsum("vjq,kj->vqk", field_now, band_interp, precision=HIGH).reshape(
        level_here, tile_count, 2 * coarse_rows, window
    )
    own_window = (
        (frac_every * rows_window)
        .reshape(level_here, tile_count, coarse_rows, 2, window)
        .sum(axis=3)
    )
    above_window = (
        ((1.0 - frac_every) * rows_window)
        .reshape(level_here, tile_count, coarse_rows, 2, window)
        .sum(axis=3)
    )
    extended_adjoint = jnp.pad(own_window, ((0, 0), (0, 0), (0, 1), (0, 0))) + jnp.pad(
        above_window, ((0, 0), (0, 0), (1, 0), (0, 0))
    )
    returned = lax.all_to_all(extended_adjoint, "tile", split_axis=1, concat_axis=1, tiled=True)
    column_sums = jnp.einsum("vnrk,cnk->vrc", returned, select, precision=HIGH)
    base_part = column_sums[:, :coarse_rows, :]
    edge_row = column_sums[:, coarse_rows:, :]
    carried = shifted(edge_row, "tile", 1)
    increment_adjoint = base_part + jnp.concatenate(
        [carried, jnp.zeros((level_here, coarse_rows - 1, col_count), jnp.float32)], axis=1
    )
    member_adjoint = spread * jnp.einsum(
        "mvrc,vrc->rmvc", perturbations.astype(jnp.float32), increment_adjoint, precision=HIGH
    )

    def backward_row(pair_now, inputs):
        gain_now, stretch = pair_now
        rate_row, row_vals = inputs
        outputs_here = (gain_now, stretch)
        gain_now = rate_row * gain_now
        stretch = rate_row[None, :, None] * (row_vals + stretch)
        return ((gain_now, stretch), outputs_here)

    summary_up, (gains_up, stretches_up) = lax.scan(
        backward_row, start_pair, (filter_rate, member_adjoint), reverse=True
    )
    _, incoming_up = carried_in(summary_up, "tile", compose, start_pair, True)
    summed = member_adjoint + gains_up[:, None, :, None] * incoming_up[None] + stretches_up
    scaled = summed * shrink[:, None, :, None]
    return control + jnp.einsum("rmvd,cd->mvrc", scaled, filter_table, precision=HIGH)

def split(x):
    high = x.astype(jnp.bfloat16)
    return high, (x - high.astype(jnp.float32)).astype(jnp.bfloat16)


def product(a, b, turned):
    dims = (((1,), (1 if turned else 0,)), ((), ()))

    def one(left, right):
        return lax.dot_general(left, right, dims, preferred_element_type=jnp.float32)

    total = None
    for i, left in enumerate(a):
        for j, right in enumerate(b):
            if i + j < 2:
                term = one(left, right)
                total = term if total is None else total + term
    return total


def expand(ref, count):
    return jnp.concatenate(
        [jnp.broadcast_to(ref[q : q + 1, :], (8, 128))[None] for q in range(count)], axis=0
    )


def wide(x):
    pad = jnp.zeros(x.shape[:-1] + (128 - x.shape[-1],), x.dtype)
    return jnp.concatenate([x, pad], axis=x.ndim - 1)


def placed_at(x, source, target, width):
    moved = pltpu.roll(x, (target - source) % 128, 1)
    lane = lax.broadcasted_iota(jnp.int32, x.shape, 1)
    return jnp.where((lane >= target) & (lane < target + width), moved, 0.0)


def column(row):
    count = row.shape[1]
    sub = lax.broadcasted_iota(jnp.int32, (count, count), 0)
    lane = lax.broadcasted_iota(jnp.int32, (count, count), 1)
    return jnp.sum(jnp.where(sub == lane, row, 0.0), axis=1, keepdims=True)


def hessian_kernel(
    tiles, mems, spread,
    ctl_hbm, prt_hbm, rates_hbm, lat_hbm, lon_hbm, east_hbm, north_hbm, obs_hbm,
    out,
    ctl, prt, rates, lat_in, lon_in, east_in, north_in, obs_in,
    small, smalls, halo_out, halo_in, wind_rows, weights, send_a, got_a, send_b, got_b,
    parts, parts_got, rows_out, rows_in, adj_out, adj_in, own_adj, adj_all,
    send_c, got_c, send_d, got_d, interp,
    local_sem, halo_send, halo_recv, tile_send, tile_recv, mem_send, mem_recv,
):
    members, rows, levels, cols = ctl.shape
    t = lax.axis_index("tile")
    m = lax.axis_index("mem")
    f32 = jnp.float32
    started = []
    group_levels = levels // mems
    rows_fine, band = east_in.shape
    halo = 2 * STEPS
    width = band + 2 * halo
    slots = send_a.shape[1]
    chunks = [(i, min(i + CHUNK, slots)) for i in range(0, slots, CHUNK)]
    ends = [min(members, 256 * high // cols) for low, high in chunks[:-1]] + [members]
    sets = list(zip([0] + ends[:-1], ends))

    loads = []
    sources = (
        (rates_hbm, rates), (ctl_hbm, ctl), (lat_hbm, lat_in), (east_hbm, east_in),
        (north_hbm, north_in), (obs_hbm.at[pl.ds(m * group_levels, group_levels)], obs_in),
        (lon_hbm, lon_in), (prt_hbm, prt),
    )
    for i, (source, target) in enumerate(sources):
        load = pltpu.make_async_copy(source, target, local_sem.at[i])
        load.start()
        loads.append(load)

    barrier = pltpu.get_barrier_semaphore()
    for d in range(1, tiles):
        pl.semaphore_signal(
            barrier, inc=1, device_id={"tile": lax.rem(t + d, tiles)}, device_id_type=MESH
        )
    for d in range(1, mems):
        pl.semaphore_signal(
            barrier, inc=1, device_id={"mem": lax.rem(m + d, mems)}, device_id_type=MESH
        )

    def spread_out(kind, axis, source, target, place=lambda ref, me: ref.at[me]):
        size, me = (tiles, t) if axis == "tile" else (mems, m)
        sends, recvs = (tile_send, tile_recv) if axis == "tile" else (mem_send, mem_recv)
        copies = []
        for d in range(1, size):
            dest = lax.rem(me + d, size)
            copy = pltpu.make_async_remote_copy(
                src_ref=source(dest),
                dst_ref=place(target, me),
                send_sem=sends.at[kind, d],
                recv_sem=recvs.at[kind, d],
                device_id={axis: dest},
                device_id_type=MESH,
            )
            copy.start()
            copies.append(copy)
        place(target, me)[...] = source(me)[...]
        started.extend(copies)
        return copies

    def exchange(kind, chunk, source, target):
        low, high = chunks[chunk]
        span = pl.ds(low, high - low)
        return spread_out(
            3 + kind * len(chunks) + chunk,
            "tile",
            lambda dest: source.at[dest, span],
            target,
            lambda ref, me: ref.at[me, span],
        )

    def arrive(copies):
        for copy in copies:
            copy.wait_recv()

    groups = levels // 8
    half = cols // 2

    def store_pieces(target, value):
        for side in range(2):
            lanes = [x[:, side * half : (side + 1) * half] for x in value]
            spare = slots * 128 - members * half
            if spare:
                lanes.append(jnp.zeros((levels, spare), f32))
            row = jnp.concatenate(lanes, axis=1)
            for group in range(groups):
                for k in range(slots):
                    target[side * groups + group, k] = row[
                        8 * group : 8 * group + 8, 128 * k : 128 * k + 128
                    ]

    def load_pieces(source, low, high):
        first, last = low * half // 128, -(-high * half // 128)
        sides = []
        for side in range(2):
            row = jnp.concatenate(
                [
                    jnp.concatenate(
                        [source[side * groups + g, k] for g in range(groups)], axis=0
                    )
                    for k in range(first, last)
                ],
                axis=1,
            )
            sides.append(row)
        value = []
        for i in range(low, high):
            at = i * half - 128 * first
            value.append(
                jnp.concatenate([row[:, at : at + half] for row in sides], axis=1)[None]
            )
        return jnp.concatenate(value, axis=0)

    loads[0].wait()
    rate = [column(rates[r : r + 1, :]) for r in range(rows)]
    shrink = [jnp.sqrt(1.0 - a * a) for a in rate]
    gain_row = rates[0:1, :]
    for r in range(1, rows):
        gain_row = gain_row * rates[r : r + 1, :]
    loads[2].wait()
    small[...] = jnp.zeros_like(small)
    small[0 : 2 * rows, :] = jnp.broadcast_to(
        column(lat_in[...].astype(f32)) / 256.0, (2 * rows, 128)
    )
    small[2 * rows : 2 * rows + 1, :] = wide(gain_row)

    pl.semaphore_wait(barrier, tiles - 1 + mems - 1)
    small_copies = spread_out(0, "tile", lambda dest: small, smalls)
    loads[1].wait()
    local_rows = []
    state = None
    for r in range(rows):
        term = shrink[r] * ctl[:, r]
        state = term if r == 0 else rate[r] * state + term
        local_rows.append(state)
    store_pieces(send_a, [state[i] for i in range(members)])
    carry_copies = [exchange(0, c, send_a, got_a) for c in range(len(chunks))]

    for load in loads[3:]:
        load.wait()
    east_own = wide(east_in[...].astype(f32) / 1024.0)
    north_own = wide(north_in[...].astype(f32) / 1024.0)
    edges = jnp.zeros((rows_fine, 128), f32)
    for i, wind in enumerate((east_own, north_own)):
        edges = edges + placed_at(wind, 0, 2 * halo * i, halo)
        edges = edges + placed_at(wind, band - halo, 2 * halo * i + halo, halo)
    base = 4 * halo
    for level in range(group_levels):
        slab = wide(obs_in[level])
        at = base + 2 * STEPS * level
        edges = edges + placed_at(slab, 0, at, STEPS)
        edges = edges + placed_at(slab, band - STEPS, at + STEPS, STEPS)
    halo_out[...] = edges
    halo_copies = []
    for side, d in enumerate((1, tiles - 1)):
        copy = pltpu.make_async_remote_copy(
            src_ref=halo_out,
            dst_ref=halo_in.at[side],
            send_sem=halo_send.at[side],
            recv_sem=halo_recv.at[side],
            device_id={"tile": lax.rem(t + d, tiles)},
            device_id_type=MESH,
        )
        copy.start()
        halo_copies.append(copy)
    started.extend(halo_copies)

    sub = lax.broadcasted_iota(jnp.int32, (cols, cols), 0)
    lane = lax.broadcasted_iota(jnp.int32, (cols, cols), 1)
    apart = (lane - sub).astype(f32)
    powers = jnp.exp(jnp.maximum(apart, 0.0) * math.log(LON_RATE))
    table = split(jnp.where(lane >= sub, math.sqrt(1.0 - LON_RATE**2) * powers, 0.0))

    def smooth(x, turned):
        flat = x.reshape(x.shape[0] * levels, cols)
        return product(split(flat), table, turned).reshape(x.shape)

    smooth_rows = [smooth(x, False) for x in local_rows]

    arrive(small_copies)
    group = lax.rem(t, levels // 8)
    lane = lax.broadcasted_iota(jnp.int32, (8, 128), 1)
    sub = lax.broadcasted_iota(jnp.int32, (8, 128), 0)
    gain_mask = lane == sub + 8 * group
    gains = []
    for s in range(tiles):
        row = smalls[s, 2 * rows : 2 * rows + 1, :]
        gains.append(jnp.sum(jnp.where(gain_mask, row, 0.0), axis=1, keepdims=True))
    back_copies = []
    for c, (low, high) in enumerate(chunks):
        arrive(carry_copies[c])
        state = jnp.zeros((high - low, 8, 128), f32)
        for s in range(tiles):
            send_b[s, low:high] = state
            state = gains[s] * state + got_a[s, low:high]
        back_copies.append(exchange(1, c, send_b, got_b))

    count = lon_in.shape[0]
    lon_row = jnp.broadcast_to(lon_in[...].astype(f32)[None] / 256.0, (8, count))
    slot = lax.broadcasted_iota(jnp.int32, (cols, 128), 0)
    lane = lax.broadcasted_iota(jnp.int32, (cols, 128), 1)
    for i in range(tiles):
        west = pltpu.roll(lon_row, (halo - band * i) % count, 1)[0:1, :128]
        lower = lax.rem(lane + (band * i - halo + count), count) // 2
        upper = lax.rem(lower + 1, cols)
        weight = jnp.where(slot == lower, west, 0.0) + jnp.where(slot == upper, 1.0 - west, 0.0)
        weight = jnp.where(lane < width, weight, 0.0)
        interp[:, 128 * i : 128 * (i + 1)] = weight.astype(jnp.bfloat16)
    arrive(halo_copies)
    from_west, from_east = halo_in[0], halo_in[1]
    for i, wind in enumerate((east_own, north_own)):
        wind_rows[i] = (
            placed_at(wind, 0, halo, band)
            + placed_at(from_west, (2 * i + 1) * halo, 0, halo)
            + placed_at(from_east, 2 * i * halo, halo + band, halo)
        )
    slabs = []
    for level in range(group_levels):
        at = base + 2 * STEPS * level
        slab = placed_at(wide(obs_in[level]), 0, halo, band)
        slab = slab + placed_at(from_west, at + STEPS, halo - STEPS, STEPS)
        slab = slab + placed_at(from_east, at, halo + band, STEPS)
        slabs.append(slab[None])
    weights[...] = jnp.swapaxes(jnp.concatenate(slabs, axis=0), 0, 1)

    partial = [jnp.zeros((levels, cols), f32)] * rows
    for c, (low, high) in enumerate(sets):
        arrive(back_copies[c])
        carried = smooth(load_pieces(got_b, low, high), False)
        gain = None
        for r in range(rows):
            gain = rate[r] if r == 0 else gain * rate[r]
            localized = gain * carried + smooth_rows[r][low:high]
            partial[r] = partial[r] + jnp.sum(prt[low:high, r].astype(f32) * localized, axis=0)
    for r in range(rows):
        for i in range(mems):
            parts[i, 8 * r : 8 * r + 8] = (
                spread * partial[r][i * group_levels : (i + 1) * group_levels]
            )
    part_copies = spread_out(0, "mem", lambda dest: parts.at[dest], parts_got)
    east = expand(wind_rows.at[0], rows_fine)
    north = expand(wind_rows.at[1], rows_fine)
    east_pos = jnp.maximum(east, 0.0)
    east_neg = jnp.maximum(-east, 0.0)
    north_pos = jnp.maximum(north, 0.0)
    north_neg = jnp.maximum(-north, 0.0)
    keep = 1.0 - east_pos - east_neg - north_pos - north_neg
    lat = jnp.concatenate([expand(smalls.at[s], 2 * rows) for s in range(tiles)], axis=0)
    arrive(part_copies)
    total = parts_got[0]
    for i in range(1, mems):
        total = total + parts_got[i]
    every = product(split(total), (interp[...],), False)
    for i in range(tiles):
        for r in range(0, rows, 2):
            block = every[8 * r : 8 * r + 8, 128 * i : 128 * (i + 1)]
            if r + 1 < rows:
                other = every[8 * r + 8 : 8 * r + 16, 128 * i : 128 * (i + 1)]
                block = block + pltpu.roll(other, 64, 1)
            rows_out[i, 4 * r : 4 * r + 8] = block
    row_copies = spread_out(1, "tile", lambda dest: rows_out.at[dest], rows_in)
    arrive(row_copies)

    coarse = tiles * rows
    edge = jnp.zeros((1, 8, 128), f32)

    def southward(x):
        return jnp.concatenate([edge, x[:-1]], axis=0)

    def northward(x):
        return jnp.concatenate([x[1:], edge], axis=0)

    def doubled(x):
        return jnp.broadcast_to(x[:, None], (coarse, 2, 8, 128)).reshape(rows_fine, 8, 128)

    def paired(x):
        pairs = x.reshape(coarse, 2, 8, 128)
        return pairs[:, 0] + pairs[:, 1]

    def turn(x, distance):
        flat = x.reshape(rows_fine * 8, 128)
        return pltpu.roll(flat, distance, 1).reshape(rows_fine, 8, 128)

    def unpacked(ref, i, r):
        block = ref[i, 8 * (r // 2) : 8 * (r // 2) + 8]
        return pltpu.roll(block, 64, 1) if r % 2 else block

    increment = jnp.concatenate(
        [unpacked(rows_in, i, r)[None] for i in range(tiles) for r in range(rows)], axis=0
    )
    g = lat * doubled(increment) + (1.0 - lat) * doubled(northward(increment))
    for _ in range(STEPS):
        g = (
            keep * g
            + east_pos * turn(g, 1)
            + east_neg * turn(g, 127)
            + north_pos * southward(g)
            + north_neg * northward(g)
        )
    g = weights[...] * g
    for _ in range(STEPS):
        g = (
            keep * g
            + turn(east_pos * g, 127)
            + turn(east_neg * g, 1)
            + northward(north_pos * g)
            + southward(north_neg * g)
        )
    lane = lax.broadcasted_iota(jnp.int32, g.shape, 2)
    g = jnp.where((lane >= halo) & (lane < halo + band), g, 0.0)
    adjoint = paired(lat * g) + southward(paired((1.0 - lat) * g))
    for i in range(tiles):
        for r in range(0, rows, 2):
            block = adjoint[i * rows + r]
            if r + 1 < rows:
                block = block + pltpu.roll(adjoint[i * rows + r + 1], 64, 1)
            adj_out[i, 4 * r : 4 * r + 8] = block
    adj_copies = spread_out(2, "tile", lambda dest: adj_out.at[dest], adj_in)
    arrive(adj_copies)
    every = jnp.concatenate(
        [
            jnp.concatenate([unpacked(adj_in, i, r) for i in range(tiles)], axis=1)
            for r in range(rows)
        ],
        axis=0,
    )
    own_adj[...] = product(split(every), (interp[...],), True)
    own_copies = spread_out(1, "mem", lambda dest: own_adj, adj_all)
    arrive(own_copies)

    fields = []
    for r in range(rows):
        field = jnp.concatenate([adj_all[i, 8 * r : 8 * r + 8] for i in range(mems)], axis=0)
        fields.append(spread * field)
    summed = []
    state = None
    for r in reversed(range(rows)):
        term = fields[r] * prt[:, r].astype(f32)
        state = term if r == rows - 1 else term + rate[r + 1] * state
        summed.insert(0, state)
    carry = rate[0] * state
    store_pieces(send_c, [carry[i] for i in range(members)])
    up_copies = [exchange(2, c, send_c, got_c) for c in range(len(chunks))]
    smooth_rows = [smooth(shrink[r] * summed[r], True) for r in range(rows)]
    last_copies = []
    for c, (low, high) in enumerate(chunks):
        arrive(up_copies[c])
        state = jnp.zeros((high - low, 8, 128), f32)
        for s in reversed(range(tiles)):
            send_d[s, low:high] = state
            state = gains[s] * state + got_c[s, low:high]
        last_copies.append(exchange(3, c, send_d, got_d))
    for c, (low, high) in enumerate(sets):
        arrive(last_copies[c])
        carried = smooth(load_pieces(got_d, low, high), True)
        gain = None
        for r in reversed(range(rows)):
            gain = jnp.ones_like(rate[r]) if r == rows - 1 else gain * rate[r + 1]
            out[low:high, r] = smooth_rows[r][low:high] + (shrink[r] * gain) * carried
    for copy in started:
        copy.wait_send()


def fused(
    perturbations, control, filter_rate, lat_weight, lon_weight, wind_east, wind_north, obs_weight
):
    members, levels, rows, cols = control.shape
    tiles, mems = lax.axis_size("tile"), lax.axis_size("mem")
    f32, i32 = jnp.float32, jnp.int32
    rows_fine, band = wind_east.shape
    ctl = jnp.transpose(control, (0, 2, 1, 3))
    prt = jnp.transpose(perturbations, (0, 2, 1, 3))
    group = levels // mems
    spread = float(1.0 / np.sqrt(np.float32(members * mems - 1)))
    slots = -(-members * (cols // 2) // 128)
    kinds = 3 + 4 * -(-slots // CHUNK)
    piece = pltpu.VMEM((tiles, slots, 8, 128), f32)
    partial = pltpu.VMEM((mems, rows * group, cols), f32)
    window = pltpu.VMEM((tiles, -(-rows // 2) * group, 128), f32)
    result = pl.pallas_call(
        functools.partial(hessian_kernel, tiles, mems, spread),
        out_shape=jax.ShapeDtypeStruct(ctl.shape, f32),
        in_specs=[pl.BlockSpec(memory_space=pltpu.HBM)] * 8,
        out_specs=pl.BlockSpec(memory_space=pltpu.VMEM),
        scratch_shapes=[
            pltpu.VMEM(ctl.shape, f32),
            pltpu.VMEM(prt.shape, prt.dtype),
            pltpu.VMEM(filter_rate.shape, f32),
            pltpu.VMEM((1, lat_weight.shape[0]), i32),
            pltpu.VMEM(lon_weight.shape, i32),
            pltpu.VMEM((rows_fine, band), i32),
            pltpu.VMEM((rows_fine, band), i32),
            pltpu.VMEM((group, rows_fine, band), f32),
            pltpu.VMEM((8, 128), f32),
            pltpu.VMEM((tiles, 8, 128), f32),
            pltpu.VMEM((rows_fine, 128), f32),
            pltpu.VMEM((2, rows_fine, 128), f32),
            pltpu.VMEM((2, rows_fine, 128), f32),
            pltpu.VMEM((rows_fine, group, 128), f32),
            *[piece] * 4,
            *[partial] * 2,
            *[window] * 4,
            pltpu.VMEM((rows * group, cols), f32),
            partial,
            *[piece] * 4,
            pltpu.VMEM((cols, tiles * 128), jnp.bfloat16),
            pltpu.SemaphoreType.DMA((8,)),
            pltpu.SemaphoreType.DMA((2,)),
            pltpu.SemaphoreType.DMA((2,)),
            pltpu.SemaphoreType.DMA((kinds, tiles)),
            pltpu.SemaphoreType.DMA((kinds, tiles)),
            pltpu.SemaphoreType.DMA((2, mems)),
            pltpu.SemaphoreType.DMA((2, mems)),
        ],
        compiler_params=pltpu.CompilerParams(
            collective_id=0, has_side_effects=True, vmem_limit_bytes=60 * 2**20
        ),
    )(
        ctl, prt, filter_rate, lat_weight[None], lon_weight, wind_east, wind_north,
        obs_weight,
    )
    return control + jnp.transpose(result, (0, 2, 1, 3))


def plan(
    perturbations, control, filter_rate, lat_weight, lon_weight, wind_east, wind_north, obs_weight
):
    levels, rows, cols = control.shape[1:]
    tiles, mems = lax.axis_size("tile"), lax.axis_size("mem")
    rows_fine, band = wind_east.shape
    fits = (
        levels == 8 * mems
        and levels // 8 * 2 == tiles
        and cols % 2 == 0
        and tiles > 2
        and 2 * rows + 1 <= 8
        and rows_fine == 2 * rows * tiles
        and rows_fine % 8 == 0
        and 2 * STEPS <= band <= 64 - 4 * STEPS
        and levels <= 128
    )
    return (fused if fits else local)(
        perturbations, control, filter_rate, lat_weight, lon_weight, wind_east, wind_north,
        obs_weight,
    )


def solution(mesh):
    placed = (
        P("mem", None, "tile", None),
        P("mem", None, "tile", None),
        P("tile", None),
        P("tile"),
        P(),
        P(None, "tile"),
        P(None, "tile"),
        P(None, None, "tile"),
    )
    return jax.shard_map(
        plan, mesh=mesh, in_specs=placed, out_specs=P("mem", None, "tile", None), check_vma=False
    )
```
